512 devices in a mesh: seq: 64 (over x, z_lo, core), dp: 8 (over z_hi, y).
Axes of the slice: x: 4, y: 4, z: 16 (z_hi: 2, z_lo: 8; z = z_hi * 8 + z_lo), core: 2. Of those that a mesh axis runs over, the one named last changes fastest.
Arguments:
- bases: int32 [8, 32768], P('dp', 'seq'), may hold values from 0 to 3
- w_embed: bfloat16 [60, 768], replicated, may hold values from -1.5 to 1.5
- b_embed: float32 [768], replicated, may hold values from -3 to 3
- gain: float32 [768], replicated, may hold values from 0.25 to 1.75
- taps: float32 [3, 768], replicated, may hold values from -3.5 to 3.5
- w_widen: bfloat16 [768, 896], replicated, may hold values from -0.21875 to 0.21875
- cotangent: bfloat16 [8, 16384, 896], P('dp', 'seq'), may hold values from -0.109375 to 0.109375
Outputs:
- grad_embed: float32 [60, 768], replicated
- grad_bias: float32 [768], replicated
- grad_gain: float32 [768], replicated
- grad_taps: float32 [3, 768], replicated
- grad_widen: float32 [768, 896], P('dp', 'seq')
The draws below stay inside these ranges and needn't reach their ends.
All inputs are finite; a program needn't handle non-finite values.
Results may differ from the reference program's by a relative error of at most 0.007.
Values may be sent and summed in bfloat16 or wider, within the bound.
A program may use at most 128 MiB of HBM per device.

```python
import jax
import jax.numpy as jnp
from jax import lax

C0 = 768
C1 = 896
KE = 15
DILATION_STEP = 64
SEQS = 8
LENGTH = 32768
POOLED = 16384


def with_ends(array, stream_key, least, top_value):
    spot = [jax.random.randint(jax.random.fold_in(stream_key, axis), (), 0, length) for axis, length in enumerate(array.shape)]
    longest = array.shape.index(max(array.shape))
    beside = spot[:longest] + [(spot[longest] + 1) % array.shape[longest]] + spot[longest + 1:]
    return array.at[tuple(spot)].set(least).at[tuple(beside)].set(top_value)


def raised(result, own_key, source, target, shards_of, factor):
    owner, partner = [(jnp.arange(result.shape[axis_at]) // (result.shape[axis_at] // shards_of)).reshape([-1 if axis == axis_at else 1 for axis in range(result.ndim)]) for axis_at in (source, target)]
    chosen = jax.random.permutation(own_key, shards_of)[partner]
    strong = (owner == chosen) | (owner == (partner + shards_of // 2) % shards_of)
    return jnp.where(strong, factor * result, result)


def block_scale(stream_key, shape, shards, low, top_value):
    factor_of = 1.0
    for dim, shards_of in shards:
        draws = jax.random.uniform(jax.random.fold_in(jax.random.fold_in(stream_key, 6), dim), (shards_of,), jnp.float32, low / len(shards), top_value / len(shards))
        factor_of = factor_of * jnp.repeat(jnp.exp(draws), shape[dim] // shards_of).reshape((-1,) + (1,) * (len(shape) - 1 - dim))
    return factor_of


def centred(rng, dims, deviation, most, pieces=(), held_as=jnp.bfloat16):
    values = deviation * jax.random.normal(rng, dims, jnp.float32)
    if pieces:
        values = values * block_scale(rng, dims, pieces, -0.22, 0.18)
    return jnp.clip(values, -most, most).astype(held_as)


def gaussian_with(stream_key, extent, deviation, bound, shards, heavy, held_as=jnp.bfloat16):
    values = deviation * jax.random.normal(stream_key, extent, jnp.float32)
    if shards:
        values = values * block_scale(stream_key, extent, shards, -0.22, 0.18)
    return jnp.clip(raised(values, jax.random.fold_in(stream_key, 3), *heavy), -bound, bound).astype(held_as)


def setup_inputs(seed: int = 0) -> dict:
    keys = jax.random.split(jax.random.key(seed), 8)
    bases = with_ends(jax.random.randint(keys[0], (SEQS, LENGTH), 0, 4), jax.random.fold_in(keys[0], 1), 0, 3).astype(jnp.int32)
    w_embed = centred(keys[1], (KE * 4, C0), KE ** -0.5, 1.5)
    b_embed = centred(keys[2], (C0,), 0.5, 3.0, (), jnp.float32)
    gain = jnp.clip(1.0 + 0.15 * jax.random.normal(keys[3], (C0,), jnp.float32), 0.25, 1.75)
    taps = centred(keys[4], (3, C0), 3 ** -0.5, 3.5, (), jnp.float32)
    w_widen = centred(keys[5], (C0, C1), C0 ** -0.5, 0.21875)
    cotangent = gaussian_with(keys[6], (SEQS, POOLED, C1), ((POOLED * SEQS) ** -0.5), 0.109375, ((0, 8), (1, 64)), (1, 2, 64, 4.0))
    return {"bases": bases, "w_embed": w_embed, "b_embed": b_embed, "gain": gain, "taps": taps, "w_widen": w_widen, "cotangent": cotangent}


def make_patches(extended, length):
    window = jnp.stack([extended[j:j + length] for j in range(KE)], axis=1)
    table = window[:, :, None] == jnp.arange(1, 5, dtype=jnp.int32)[None, None, :]
    return table.reshape(length, KE * 4).astype(jnp.bfloat16)

def norm_gelu(value_entries, gain):
    meansq = lax.optimization_barrier(jnp.mean(value_entries * value_entries, axis=-1, keepdims=True))
    return jax.nn.gelu(value_entries * lax.rsqrt(meansq + 1e-06) * gain)

def dilated(padded_input, kernel_rows, element_count):
    grand_total = kernel_rows[1] * padded_input[DILATION_STEP:DILATION_STEP + element_count].astype(jnp.float32)
    grand_total = grand_total + kernel_rows[0] * padded_input[0:element_count].astype(jnp.float32)
    return grand_total + kernel_rows[2] * padded_input[2 * DILATION_STEP:2 * DILATION_STEP + element_count].astype(jnp.float32)

def transposed(padded_input, kernel_rows, element_count):
    grand_total = kernel_rows[1] * padded_input[DILATION_STEP:DILATION_STEP + element_count].astype(jnp.float32)
    grand_total = grand_total + kernel_rows[0] * padded_input[2 * DILATION_STEP:2 * DILATION_STEP + element_count].astype(jnp.float32)
    return grand_total + kernel_rows[2] * padded_input[0:element_count].astype(jnp.float32)

def tap_sums(grad, padded_input, element_count):
    float_gradient = grad.astype(jnp.float32)
    return jnp.stack([lax.optimization_barrier(jnp.sum(float_gradient * padded_input[kernel_position * DILATION_STEP:kernel_position * DILATION_STEP + element_count].astype(jnp.float32), axis=0)) for kernel_position in range(3)])

def one_sequence(carry, items, w_embed, b_embed, gain, taps, w_widen):
    bases_row, cot = items
    length = bases_row.shape[0]
    element_count = length // 2
    width = w_embed.shape[1]
    extended = jnp.pad(bases_row + 1, (KE // 2, KE // 2))
    patches = make_patches(extended, length)
    embedded = jnp.dot(patches, w_embed, preferred_element_type=jnp.float32) + b_embed
    pooled = (lax.optimization_barrier(jnp.sum(embedded.reshape(element_count, 2, width), axis=1)) * 0.5).astype(jnp.bfloat16)
    act_f, pull = jax.vjp(norm_gelu, pooled.astype(jnp.float32), gain)
    activation_rows = act_f.astype(jnp.bfloat16)
    activation_padded = jnp.pad(activation_rows, ((DILATION_STEP, DILATION_STEP), (0, 0)))
    mixed = dilated(activation_padded, taps, element_count)
    block = (pooled.astype(jnp.float32) + mixed).astype(jnp.bfloat16)
    g_widen = jnp.dot(block.T, cot, preferred_element_type=jnp.float32)
    block_gradient = jnp.dot(cot, w_widen.T, preferred_element_type=jnp.float32).astype(jnp.bfloat16)
    padded_gradient = jnp.pad(block_gradient, ((DILATION_STEP, DILATION_STEP), (0, 0)))
    g_taps = tap_sums(block_gradient, activation_padded, element_count)
    d_act = transposed(padded_gradient, taps, element_count)
    d_norm, g_gain = pull(d_act)
    half = ((block_gradient.astype(jnp.float32) + d_norm) * 0.5).astype(jnp.bfloat16)
    paired = lax.optimization_barrier(jnp.sum(patches.reshape(element_count, 2, KE * 4), axis=1)).astype(jnp.bfloat16)
    g_embed = jnp.dot(paired.T, half, preferred_element_type=jnp.float32)
    g_bias = 2.0 * lax.optimization_barrier(jnp.sum(half.astype(jnp.float32), axis=0))
    new = (carry[0] + g_embed, carry[1] + g_bias, carry[2] + g_gain, carry[3] + g_taps, carry[4] + g_widen)
    return (new, None)

def reference(bases, w_embed, b_embed, gain, taps, w_widen, cotangent):
    width = w_embed.shape[1]
    start = (jnp.zeros((KE * 4, width), jnp.float32), jnp.zeros((width,), jnp.float32), jnp.zeros((width,), jnp.float32), jnp.zeros((3, width), jnp.float32), jnp.zeros((width, w_widen.shape[1]), jnp.float32))

    def step(carry, items):
        return one_sequence(carry, items, w_embed, b_embed, gain, taps, w_widen)
    final, unused = lax.scan(step, start, (bases, cotangent))
    return (final[0], final[1], final[2], final[3], final[4])
```

```python
import functools

import jax
import jax.numpy as jnp
from jax import lax
from jax.experimental import pallas as pl
from jax.experimental.pallas import tpu as pltpu
from jax.sharding import PartitionSpec as P

KE = 15
DILATION_STEP = 64
C0 = 768
C1 = 896
MESH = pl.DeviceIdType.MESH
BF = jnp.bfloat16
F32 = jnp.float32
ORDER = (2, 1, 3, 0)


def device(x, y, z, core):
    return {"seq": (x * 8 + z % 8) * 2 + core, "dp": (z // 8) * 4 + y}


def reduce_kernel(
    own, oth, wid, sml,
    crecv, send1, recv1, acc1, send2, recv2, acc2,
    zsend, zrecv, ssend, srecv, fin, part,
    csem_s, csem_r, s1s, s1r, s2s, s2r, zs, zr, ss, sr, gs, gr,
):
    seq = lax.axis_index("seq")
    dp = lax.axis_index("dp")
    core = seq % 2
    x = seq // 16
    y = dp % 4
    z = (dp // 4) * 8 + (seq // 2) % 8
    zlo = z % 8
    other = 1 - core

    barrier = pltpu.get_barrier_semaphore()
    plane = [(dc, dx, dy) for dc in range(2) for dx in range(4) for dy in range(4)][1:]

    def signal(dev):
        pl.semaphore_signal(barrier, inc=1, device_id=dev, device_id_type=MESH)

    for dc, dx, dy in plane:
        signal(device((x + dx) % 4, (y + dy) % 4, z, (core + dc) % 2))
    for dz in range(1, 16):
        signal(device(x, y, (z + dz) % 16, core))
    from_y = zlo // 2

    @pl.when(from_y != y)
    def _():
        for k in range(16):
            signal(device(x, from_y, k, core))

    pl.semaphore_wait(barrier, 31 + 15 + 12)

    core_copies = []
    for o in ORDER:
        for h in range(2):
            tgt = (x + o) % 4 if h == 0 else (y + o) % 4
            c = pltpu.make_async_remote_copy(
                src_ref=oth.at[h, tgt], dst_ref=crecv.at[h, o],
                send_sem=csem_s.at[h, o], recv_sem=csem_r.at[h, o],
                device_id=device(x, y, z, other), device_id_type=MESH,
            )
            c.start()
            core_copies.append((o, h, tgt, c))

    copies1 = {}
    for o, h, tgt, c in core_copies:
        c.wait_recv()
        total = own[h, tgt] + crecv[h, o].astype(F32)
        if o == 0:
            acc1[h] = total
        else:
            send1[h, o - 1] = total.astype(BF)
            dev = device(tgt, y, z, core) if h == 0 else device(x, tgt, z, core)
            r = pltpu.make_async_remote_copy(
                src_ref=send1.at[h, o - 1], dst_ref=recv1.at[h, o - 1],
                send_sem=s1s.at[h, o - 1], recv_sem=s1r.at[h, o - 1],
                device_id=dev, device_id_type=MESH,
            )
            r.start()
            copies1[h, o] = r

    copies2 = {}
    for h in range(2):
        for o in (1, 3, 2):
            copies1[h, o].wait_recv()
        for o in ORDER:
            tgt = (y + o) % 4 if h == 0 else (x + o) % 4
            total = acc1[h, tgt]
            for k in range(3):
                total = total + recv1[h, k, tgt].astype(F32)
            if o == 0:
                acc2[h] = total
            else:
                send2[h, o - 1] = total.astype(BF)
                dev = device(x, tgt, z, core) if h == 0 else device(tgt, y, z, core)
                r = pltpu.make_async_remote_copy(
                    src_ref=send2.at[h, o - 1], dst_ref=recv2.at[h, o - 1],
                    send_sem=s2s.at[h, o - 1], recv_sem=s2r.at[h, o - 1],
                    device_id=dev, device_id_type=MESH,
                )
                r.start()
                copies2[h, o] = r

    zcopies = []
    scopies = []
    for h in range(2):
        for o in (1, 3, 2):
            copies2[h, o].wait_recv()
        total = acc2[h]
        for k in range(3):
            total = total + recv2[h, k].astype(F32)
        if h == 0:
            for i in range(6):
                part[2 * i : 2 * i + 2, :] = total[14:16, 128 * i : 128 * i + 128]
            part[12:16, :] = jnp.zeros((4, 128), F32)
            ssend[...] = part[...].astype(BF)
            for dz in range(1, 16):
                r = pltpu.make_async_remote_copy(
                    src_ref=ssend, dst_ref=srecv.at[dz - 1],
                    send_sem=ss.at[dz - 1], recv_sem=sr.at[dz - 1],
                    device_id=device(x, y, (z + dz) % 16, core), device_id_type=MESH,
                )
                r.start()
                scopies.append(r)
        for d in range(8):
            piece = total[:, 96 * d : 96 * d + 96].astype(BF)
            zsend[h, d] = jnp.concatenate([piece, jnp.zeros((16, 32), BF)], axis=1)
            to_y, to_z = d % 4, (d // 4) * 8 + 2 * y + h
            r = pltpu.make_async_remote_copy(
                src_ref=zsend.at[h, d], dst_ref=zrecv.at[z],
                send_sem=zs.at[h * 8 + d], recv_sem=zr.at[z],
                device_id=device(x, to_y, to_z, core), device_id_type=MESH,
            )
            local = pltpu.make_async_copy(zsend.at[h, d], zrecv.at[z], zr.at[z])
            mine = jnp.logical_and(to_y == y, to_z == z)
            pl.when(mine)(local.start)
            pl.when(jnp.logical_not(mine))(r.start)
            zcopies.append((mine, r))

    total = part[...]
    for k in range(15):
        scopies[k].wait_recv()
        total = total + srecv[k].astype(F32)
    fin[...] = total
    me = (core * 4 + x) * 4 + y
    sml[me] = total
    gcopies = []
    for k, (dc, dx, dy) in enumerate(plane):
        r = pltpu.make_async_remote_copy(
            src_ref=fin, dst_ref=sml.at[me],
            send_sem=gs.at[k], recv_sem=gr.at[k],
            device_id=device((x + dx) % 4, (y + dy) % 4, z, (core + dc) % 2),
            device_id_type=MESH,
        )
        r.start()
        gcopies.append(r)

    total = jnp.zeros((16, 128), F32)
    for k in range(16):
        pltpu.make_async_remote_copy(
            src_ref=zsend.at[0, 0], dst_ref=zrecv.at[k],
            send_sem=zs.at[0], recv_sem=zr.at[k],
            device_id=device(x, y, z, other), device_id_type=MESH,
        ).wait_recv()
        total = total + zrecv[k].astype(F32)
    wid[...] = total

    for k, (dc, dx, dy) in enumerate(plane):
        slot = ((core + 2 - dc) % 2 * 4 + (x + 4 - dx) % 4) * 4 + (y + 4 - dy) % 4
        pltpu.make_async_remote_copy(
            src_ref=fin, dst_ref=sml.at[slot],
            send_sem=gs.at[k], recv_sem=gr.at[k],
            device_id=device(x, y, z, other), device_id_type=MESH,
        ).wait_recv()

    for _, _, _, c in core_copies:
        c.wait_send()
    for c in list(copies1.values()) + list(copies2.values()) + scopies + gcopies:
        c.wait_send()
    for mine, r in zcopies:
        pl.when(jnp.logical_not(mine))(r.wait_send)


def reduce_all(own, oth):
    dma = pltpu.SemaphoreType.DMA
    vmem = pl.BlockSpec(memory_space=pltpu.VMEM)
    return pl.pallas_call(
        reduce_kernel,
        out_shape=(
            jax.ShapeDtypeStruct((16, 128), F32),
            jax.ShapeDtypeStruct((32, 16, 128), F32),
        ),
        in_specs=[vmem, vmem],
        out_specs=(vmem, vmem),
        scratch_shapes=[
            pltpu.VMEM((2, 4, 4, 16, C0), BF),
            pltpu.VMEM((2, 3, 4, 16, C0), BF),
            pltpu.VMEM((2, 3, 4, 16, C0), BF),
            pltpu.VMEM((2, 4, 16, C0), F32),
            pltpu.VMEM((2, 3, 16, C0), BF),
            pltpu.VMEM((2, 3, 16, C0), BF),
            pltpu.VMEM((2, 16, C0), F32),
            pltpu.VMEM((2, 8, 16, 128), BF),
            pltpu.VMEM((16, 16, 128), BF),
            pltpu.VMEM((16, 128), BF),
            pltpu.VMEM((15, 16, 128), BF),
            pltpu.VMEM((16, 128), F32),
            pltpu.VMEM((16, 128), F32),
            dma((2, 4)), dma((2, 4)),
            dma((2, 3)), dma((2, 3)),
            dma((2, 3)), dma((2, 3)),
            dma((16,)), dma((16,)),
            dma((15,)), dma((15,)),
            dma((31,)), dma((31,)),
        ],
        compiler_params=pltpu.CompilerParams(
            collective_id=0, has_side_effects=True, vmem_limit_bytes=40 * 1024 * 1024
        ),
        name="reduce_all",
    )(own, oth)


def padded(block, sides, width):
    for axis, dim in sides:
        count = lax.axis_size(axis)
        forward = [(i, i + 1) for i in range(count - 1)]
        backward = [(target, source) for source, target in forward]
        low = lax.ppermute(
            lax.slice_in_dim(block, block.shape[dim] - width, None, axis=dim), axis, forward
        )
        high = lax.ppermute(lax.slice_in_dim(block, 0, width, axis=dim), axis, backward)
        block = jnp.concatenate([low, block, high], axis=dim)
    return block


def make_patches(extended, length):
    window = jnp.stack([extended[j : j + length] for j in range(KE)], axis=1)
    table = window[:, :, None] == jnp.arange(1, 5, dtype=jnp.int32)[None, None, :]
    return table.reshape(length, KE * 4).astype(jnp.bfloat16)


def norm_gelu(value_entries, gain):
    meansq = jnp.mean(value_entries * value_entries, axis=-1, keepdims=True)
    return jax.nn.gelu(value_entries * lax.rsqrt(meansq + 1e-06) * gain)


def shifted_sum(padded_input, rows, element_count):
    step = DILATION_STEP
    total = rows[1] * padded_input[step : step + element_count].astype(F32)
    total = total + rows[0] * padded_input[0:element_count].astype(F32)
    return total + rows[2] * padded_input[2 * step : 2 * step + element_count].astype(F32)


def tap_sums(grad, padded_input, element_count):
    g = grad.astype(F32)
    step = DILATION_STEP
    return jnp.stack(
        [
            jnp.sum(g * padded_input[k * step : k * step + element_count].astype(F32), axis=0)
            for k in range(3)
        ]
    )


def with_rims(value_entries):
    return padded(value_entries, (("seq", 0),), DILATION_STEP)


def halves(g, smalls):
    g = g.reshape(4, 4, 2, 2, 14, C0)
    g = g.transpose(3, 2, 0, 1, 4, 5)
    s = smalls.reshape(2, 1, 4, 4, 2, C0)
    s = jnp.concatenate([s, jnp.zeros_like(s)], axis=1)
    g = jnp.concatenate([g, s], axis=4)
    return jnp.stack([g[:, 0], g[:, 1].transpose(0, 2, 1, 3, 4)], axis=1)


def local(bases, w_embed, b_embed, gain, taps, w_widen, cotangent):
    length = bases.shape[1]
    element_count = length // 2
    width = w_embed.shape[1]
    extended = padded(bases + 1, (("seq", 1),), KE // 2)[0]
    patches = make_patches(extended, length)
    embedded = jnp.dot(patches, w_embed, preferred_element_type=F32) + b_embed
    pooled = (jnp.sum(embedded.reshape(element_count, 2, width), axis=1) * 0.5).astype(BF)
    act_f, pull = jax.vjp(norm_gelu, pooled.astype(F32), gain)
    activation_rows = act_f.astype(BF)
    cot = cotangent[0]
    block_gradient = lax.dot_general(
        cot, w_widen, (((1,), (1,)), ((), ())), preferred_element_type=F32
    ).astype(BF)
    activation_padded = with_rims(activation_rows)
    mixed = shifted_sum(activation_padded, taps, element_count)
    padded_gradient = with_rims(block_gradient)
    g_taps = tap_sums(block_gradient, activation_padded, element_count)
    d_act = shifted_sum(padded_gradient, taps[::-1], element_count)
    block = (pooled.astype(F32) + mixed).astype(BF)
    g = lax.dot_general(cot, block, (((0,), (0,)), ((), ())), preferred_element_type=F32)
    d_norm, g_gain = pull(d_act)
    half = ((block_gradient.astype(F32) + d_norm) * 0.5).astype(BF)
    paired = jnp.sum(patches.reshape(element_count, 2, KE * 4), axis=1)
    g_embed = lax.dot_general(
        paired, half, (((0,), (0,)), ((), ())), preferred_element_type=F32
    )
    smalls = jnp.concatenate([g_embed, g_gain[None], g_taps], axis=0)
    both = halves(g, smalls)
    core = lax.axis_index("seq") % 2
    own = lax.dynamic_index_in_dim(both, core, 0, keepdims=False)
    oth = lax.dynamic_index_in_dim(both, 1 - core, 0, keepdims=False).astype(BF)
    wid, sml = reduce_all(own, oth)
    g_widen = wid[:14, :96].T
    small = sml[:, :12].reshape(32, 6, 2, 128).transpose(0, 2, 1, 3).reshape(64, C0)
    g_embed = small[:60]
    return (g_embed, jnp.sum(g_embed[28:32], axis=0), small[60], small[61:64], g_widen)


def solution(mesh):
    return jax.shard_map(
        local,
        mesh=mesh,
        in_specs=(P("dp", "seq"), P(), P(), P(), P(), P(), P("dp", "seq", None)),
        out_specs=(P(), P(), P(), P(), P("dp", "seq")),
        check_vma=False,
    )
```

```python
import jax
import jax.numpy as jnp
from jax import lax
from jax.experimental import pallas as pl
from jax.experimental.pallas import tpu as pltpu
from jax.sharding import PartitionSpec as P

KE = 15
STEP = 64
C0 = 768
C1 = 896
BINS = 256
ROWS = BINS + 2 * STEP
TILES = 24
MESH = pl.DeviceIdType.MESH
BF = jnp.bfloat16
F32 = jnp.float32
ORDER = (2, 1, 3, 0)
PLANE = [(dc, dx, dy) for dc in range(2) for dx in range(4) for dy in range(4)][1:]
GELU_A = 0.7978845608028654
GELU_B = 0.044715


def device(x, y, z, core):
    return {"seq": (x * 8 + z % 8) * 2 + core, "dp": (z // 8) * 4 + y}


def dot(a, b, ca, cb):
    return lax.dot_general(a, b, (((ca,), (cb,)), ((), ())), preferred_element_type=F32)


def iota(shape, dim):
    return lax.broadcasted_iota(jnp.int32, shape, dim)


def chosen(shape, cond):
    return jnp.where(cond, jnp.ones(shape, F32), jnp.zeros(shape, F32)).astype(BF)


def column_choice(h, core):
    j = iota((256, 1), 0)
    a, b, i = j >> 6, (j >> 4) & 3, j & 15
    x, yq = (a, b) if h == 0 else (b, a)
    col = ((x * 8 + yq * 2 + h) * 2 + core) * 14 + i
    col = jnp.where(i < 14, col, -1)
    return chosen((256, C1), iota((256, C1), 1) == col)


def normed(pooled, gain):
    xf = pooled.astype(F32)
    rs = lax.rsqrt(jnp.mean(xf * xf, axis=-1, keepdims=True) + 1e-06)
    y = xf * rs
    n = y * gain
    t = jnp.tanh(GELU_A * (n + GELU_B * (n * n * n)))
    return rs, y, n, t


def fold(v):
    return v[0:8] + v[8:16]


def kernel(
    bases, w_embed, b_embed, gain, taps, w_widen, cot,
    o_embed, o_bias, o_gain, o_taps, o_widen,
    lb, rb, lcot, rcot, tt, paired, emb, pool, act, dblk, block, half, cot_t, sm, smb,
    own, oth, crecv, send1, recv1, acc1, send2, recv2, acc2, zsend, zrecv,
    rsrecv, part, ssend, srecv, fin, agb,
    hs, hr, csem_s, csem_r, s1s, s1r, s2s, s2r, zs, zr, rss, rsr, ss, sr, gs, gr,
):
    seq = lax.axis_index("seq")
    dp = lax.axis_index("dp")
    core = seq % 2
    x = seq // 16
    y = dp % 4
    z = (dp // 4) * 8 + (seq // 2) % 8
    other = 1 - core
    me = (core * 4 + x) * 4 + y
    reducer = me < TILES
    right = {"seq": (seq + 1) % 64, "dp": dp}
    left = {"seq": (seq + 63) % 64, "dp": dp}

    barrier = pltpu.get_barrier_semaphore()

    def signal(dev):
        pl.semaphore_signal(barrier, inc=1, device_id=dev, device_id_type=MESH)

    signal(right)
    signal(left)
    for dz in range(1, 16):
        signal(device(x, y, (z + dz) % 16, core))
    from_y = (z % 8) // 2

    @pl.when(from_y != y)
    def _():
        for k in range(16):
            signal(device(x, from_y, k, core))

    for dc, dx, dy in PLANE:
        signal(device((x + dx) % 4, (y + dy) % 4, z, (core + dc) % 2))

    def remote(src, dst, send, recv, dev):
        return pltpu.make_async_remote_copy(
            src_ref=src, dst_ref=dst, send_sem=send, recv_sem=recv,
            device_id=dev, device_id_type=MESH,
        )

    dblk[STEP : STEP + BINS] = dot(cot[0], w_widen[...], 1, 1).astype(BF)
    for w in range(2):
        for h in range(2):
            pick = column_choice(h, core if w == 0 else other)
            cot_t[w, h] = dot(pick, cot[0], 1, 1).astype(BF)

    pl.semaphore_wait(barrier, 2 + 31 + 15 + 12)

    halo = [
        remote(bases, lb, hs.at[0], hr.at[0], right),
        remote(bases, rb, hs.at[1], hr.at[1], left),
        remote(cot.at[0, pl.ds(BINS - STEP, STEP)], lcot, hs.at[2], hr.at[2], right),
        remote(cot.at[0, pl.ds(0, STEP)], rcot, hs.at[3], hr.at[3], left),
    ]
    for c in halo:
        c.start()
    halo[0].wait_recv()
    halo[1].wait_recv()

    ext = jnp.concatenate([lb[:, 256:512], bases[...], rb[:, 0:256]], axis=1)
    pos = iota((1, 1024), 1) + seq * 512 - 256
    ext = jnp.where(jnp.logical_and(pos >= 0, pos < 32768), ext, -1).astype(F32)
    for m in range(16):
        tt[m : m + 1, :] = pltpu.roll(ext, 1024 - 121 - m, 1)
    p, col = iota((C0, ROWS), 0), iota((C0, ROWS), 1)
    spot = jnp.where(col < 256, col + 64, jnp.where(col < 320, col - 256, col))
    even = chosen((C0, ROWS), p == 2 * spot)
    win = dot(tt[:, 0:C0].astype(BF), even, 1, 0).astype(BF)
    tap_of, base_of = iota((KE * 4, 16), 0) >> 2, (iota((KE * 4, ROWS), 0) & 3).astype(F32)
    at = iota((KE * 4, 16), 1)
    first = dot(chosen((KE * 4, 16), at == tap_of), win, 1, 0)
    second = dot(chosen((KE * 4, 16), at == tap_of + 1), win, 1, 0)
    one, zero = jnp.ones((KE * 4, ROWS), F32), jnp.zeros((KE * 4, ROWS), F32)
    paired[...] = (
        jnp.where(first == base_of, one, zero) + jnp.where(second == base_of, one, zero)
    ).astype(BF)
    emb[...] = dot(paired[...], w_embed[...], 0, 0)

    def forward(i, _):
        rows = pl.ds(pl.multiple_of(i * 16, 16), 16)
        v = (emb[rows] * 0.5 + b_embed[...]).astype(BF)
        pool[rows] = v
        _, _, n, t = normed(v, gain[...])
        to = pl.ds(pl.multiple_of(i * 16 + STEP, 16), 16)
        act[to] = (0.5 * n * (1.0 + t)).astype(BF)
        return 0

    lax.fori_loop(0, BINS // 16, forward, 0)
    has_left = jnp.where(seq > 0, 1.0, 0.0)
    has_right = jnp.where(seq < 63, 1.0, 0.0)

    def forward_rim(i, _):
        rows = pl.ds(pl.multiple_of(i * 16 + BINS, 16), 16)
        v = (emb[rows] * 0.5 + b_embed[...]).astype(BF)
        _, _, n, t = normed(v, gain[...])
        keep = jnp.where(i < 4, has_left, has_right)
        to = pl.ds(pl.multiple_of(jnp.where(i < 4, i * 16, i * 16 + BINS), 16), 16)
        act[to] = (0.5 * n * (1.0 + t) * keep).astype(BF)
        return 0

    lax.fori_loop(0, 8, forward_rim, 0)

    def mix(i, _):
        rows = pl.ds(pl.multiple_of(i * 16, 16), 16)
        total = pool[rows].astype(F32)
        for k in (1, 0, 2):
            from_ = pl.ds(pl.multiple_of(i * 16 + k * STEP, 16), 16)
            total = total + taps[k : k + 1] * act[from_].astype(F32)
        block[rows] = total.astype(BF)
        return 0

    lax.fori_loop(0, BINS // 16, mix, 0)

    core_copies = []
    for h in range(2):
        oth[h] = dot(cot_t[1, h], block[...], 1, 0).astype(BF).reshape(4, 4, 16, C0)
        for o in ORDER:
            tgt = (x + o) % 4 if h == 0 else (y + o) % 4
            c = remote(
                oth.at[h, tgt], crecv.at[h, o], csem_s.at[h, o], csem_r.at[h, o],
                device(x, y, z, other),
            )
            c.start()
            core_copies.append((o, h, tgt, c))
    for h in range(2):
        own[h] = dot(cot_t[0, h], block[...], 1, 0).reshape(4, 4, 16, C0)

    halo[2].wait_recv()
    halo[3].wait_recv()
    dblk[0:STEP] = (dot(lcot[...], w_widen[...], 1, 1) * has_left).astype(BF)
    dblk[STEP + BINS : ROWS] = (dot(rcot[...], w_widen[...], 1, 1) * has_right).astype(BF)

    def backward(i, sums):
        rows = pl.ds(pl.multiple_of(i * 16, 16), 16)
        at = [pl.ds(pl.multiple_of(i * 16 + k * STEP, 16), 16) for k in range(3)]
        d = dblk[at[1]].astype(F32)
        d_act = taps[1:2] * d
        d_act = d_act + taps[0:1] * dblk[at[2]].astype(F32)
        d_act = d_act + taps[2:3] * dblk[at[0]].astype(F32)
        rs, yv, n, t = normed(pool[rows], gain[...])
        slope = 0.5 * (1.0 + t) + 0.5 * n * (1.0 - t * t) * (
            GELU_A * (1.0 + 3.0 * GELU_B * (n * n))
        )
        dn = d_act * slope
        dy = dn * gain[...]
        d_norm = rs * (dy - yv * jnp.mean(dy * yv, axis=-1, keepdims=True))
        half[rows] = ((d + d_norm) * 0.5).astype(BF)
        new = [fold(dn * yv)] + [fold(d * act[at[k]].astype(F32)) for k in range(3)]
        return tuple(a + b for a, b in zip(sums, new))

    start = tuple(jnp.zeros((8, C0), F32) for _ in range(4))
    sums = lax.fori_loop(0, BINS // 16, backward, start)
    sm[0 : KE * 4] = dot(paired[:, 0:BINS], half[...], 1, 0)
    for k in range(4):
        sm[KE * 4 + k : KE * 4 + k + 1] = jnp.sum(sums[k], axis=0, keepdims=True)
    for c in range(TILES):
        i, j = c // 6, c % 6
        smb[c] = sm[16 * i : 16 * i + 16, 128 * j : 128 * j + 128].astype(BF)

    rs_copies = []
    for k in range(TILES):
        c = (me + k) % TILES
        r = remote(
            smb.at[c], rsrecv.at[me], rss.at[k], rsr.at[me],
            device((c // 4) % 4, c % 4, z, c // 16),
        )
        if k == 0:
            stay = pltpu.make_async_copy(smb.at[c], rsrecv.at[me], rsr.at[me])
            pl.when(reducer)(stay.start)
            pl.when(jnp.logical_not(reducer))(r.start)
        else:
            r.start()
        rs_copies.append(r)

    copies1 = {}
    for o, h, tgt, c in core_copies:
        c.wait_recv()
        total = own[h, tgt] + crecv[h, o].astype(F32)
        if o == 0:
            acc1[h] = total
        else:
            send1[h, o - 1] = total.astype(BF)
            dev = device(tgt, y, z, core) if h == 0 else device(x, tgt, z, core)
            r = remote(
                send1.at[h, o - 1], recv1.at[h, o - 1], s1s.at[h, o - 1], s1r.at[h, o - 1], dev
            )
            r.start()
            copies1[h, o] = r

    copies2 = {}
    for h in range(2):
        for o in (1, 3, 2):
            copies1[h, o].wait_recv()
        for o in ORDER:
            tgt = (y + o) % 4 if h == 0 else (x + o) % 4
            total = acc1[h, tgt]
            for k in range(3):
                total = total + recv1[h, k, tgt].astype(F32)
            if o == 0:
                acc2[h] = total
            else:
                send2[h, o - 1] = total.astype(BF)
                dev = device(x, tgt, z, core) if h == 0 else device(tgt, y, z, core)
                r = remote(
                    send2.at[h, o - 1], recv2.at[h, o - 1],
                    s2s.at[h, o - 1], s2r.at[h, o - 1], dev,
                )
                r.start()
                copies2[h, o] = r

    z_small = [
        remote(
            ssend, srecv.at[dz - 1], ss.at[dz - 1], sr.at[dz - 1],
            device(x, y, (z + dz) % 16, core),
        )
        for dz in range(1, 16)
    ]

    @pl.when(reducer)
    def _():
        total = jnp.zeros((16, 128), F32)
        for k in range(32):
            remote(
                smb.at[0], rsrecv.at[k], rss.at[0], rsr.at[k], device(x, y, z, other)
            ).wait_recv()
            total = total + rsrecv[k].astype(F32)
        part[...] = total
        ssend[...] = total.astype(BF)
        for r in z_small:
            r.start()

    zcopies = []
    for h in range(2):
        for o in (1, 3, 2):
            copies2[h, o].wait_recv()
        total = acc2[h]
        for k in range(3):
            total = total + recv2[h, k].astype(F32)
        for d in range(8):
            piece = total[:, 96 * d : 96 * d + 96].astype(BF)
            zsend[h, d] = jnp.concatenate([piece, jnp.zeros((16, 32), BF)], axis=1)
            to_y, to_z = d % 4, (d // 4) * 8 + 2 * y + h
            r = remote(
                zsend.at[h, d], zrecv.at[z], zs.at[h * 8 + d], zr.at[z],
                device(x, to_y, to_z, core),
            )
            stay = pltpu.make_async_copy(zsend.at[h, d], zrecv.at[z], zr.at[z])
            mine = jnp.logical_and(to_y == y, to_z == z)
            pl.when(mine)(stay.start)
            pl.when(jnp.logical_not(mine))(r.start)
            zcopies.append((mine, r))

    gcopies = [
        remote(
            fin, agb.at[me], gs.at[k], gr.at[me],
            device((x + dx) % 4, (y + dy) % 4, z, (core + dc) % 2),
        )
        for k, (dc, dx, dy) in enumerate(PLANE)
    ]

    @pl.when(reducer)
    def _():
        total = part[...]
        for k in range(15):
            z_small[k].wait_recv()
            total = total + srecv[k].astype(F32)
        fin[...] = total.astype(BF)
        agb[me] = total.astype(BF)
        for r in gcopies:
            r.start()

    total = jnp.zeros((16, 128), F32)
    for k in range(16):
        remote(
            zsend.at[0, 0], zrecv.at[k], zs.at[0], zr.at[k], device(x, y, z, other)
        ).wait_recv()
        total = total + zrecv[k].astype(F32)
    o_widen[...] = total.T[0:96, 0:14]

    for c in range(TILES):
        r = remote(fin, agb.at[c], gs.at[0], gr.at[c], device(x, y, z, other))
        pl.when(me != c)(r.wait_recv)
    for c in range(TILES):
        i, j = c // 6, c % 6
        sm[16 * i : 16 * i + 16, 128 * j : 128 * j + 128] = agb[c].astype(F32)
    o_embed[...] = sm[0 : KE * 4]
    o_bias[...] = jnp.sum(sm[28:32], axis=0, keepdims=True)
    o_gain[...] = sm[60:61]
    o_taps[...] = sm[61:64]

    for c in halo:
        c.wait_send()
    for _, _, _, c in core_copies:
        c.wait_send()
    for c in list(copies1.values()) + list(copies2.values()) + rs_copies[1:]:
        c.wait_send()
    pl.when(jnp.logical_not(reducer))(rs_copies[0].wait_send)

    @pl.when(reducer)
    def _():
        for r in z_small + gcopies:
            r.wait_send()

    for mine, r in zcopies:
        pl.when(jnp.logical_not(mine))(r.wait_send)


def local(bases, w_embed, b_embed, gain, taps, w_widen, cotangent):
    dma = pltpu.SemaphoreType.DMA
    vmem = pl.BlockSpec(memory_space=pltpu.VMEM)
    out = pl.pallas_call(
        kernel,
        out_shape=(
            jax.ShapeDtypeStruct((KE * 4, C0), F32),
            jax.ShapeDtypeStruct((1, C0), F32),
            jax.ShapeDtypeStruct((1, C0), F32),
            jax.ShapeDtypeStruct((3, C0), F32),
            jax.ShapeDtypeStruct((96, 14), F32),
        ),
        in_specs=[vmem] * 7,
        out_specs=(vmem,) * 5,
        scratch_shapes=[
            pltpu.VMEM((1, 512), jnp.int32),
            pltpu.VMEM((1, 512), jnp.int32),
            pltpu.VMEM((STEP, C1), BF),
            pltpu.VMEM((STEP, C1), BF),
            pltpu.VMEM((16, 1024), F32),
            pltpu.VMEM((KE * 4, ROWS), BF),
            pltpu.VMEM((ROWS, C0), F32),
            pltpu.VMEM((BINS, C0), BF),
            pltpu.VMEM((ROWS, C0), BF),
            pltpu.VMEM((ROWS, C0), BF),
            pltpu.VMEM((BINS, C0), BF),
            pltpu.VMEM((BINS, C0), BF),
            pltpu.VMEM((2, 2, 256, BINS), BF),
            pltpu.VMEM((64, C0), F32),
            pltpu.VMEM((TILES, 16, 128), BF),
            pltpu.VMEM((2, 4, 4, 16, C0), F32),
            pltpu.VMEM((2, 4, 4, 16, C0), BF),
            pltpu.VMEM((2, 4, 4, 16, C0), BF),
            pltpu.VMEM((2, 3, 4, 16, C0), BF),
            pltpu.VMEM((2, 3, 4, 16, C0), BF),
            pltpu.VMEM((2, 4, 16, C0), F32),
            pltpu.VMEM((2, 3, 16, C0), BF),
            pltpu.VMEM((2, 3, 16, C0), BF),
            pltpu.VMEM((2, 16, C0), F32),
            pltpu.VMEM((2, 8, 16, 128), BF),
            pltpu.VMEM((16, 16, 128), BF),
            pltpu.VMEM((32, 16, 128), BF),
            pltpu.VMEM((16, 128), F32),
            pltpu.VMEM((16, 128), BF),
            pltpu.VMEM((15, 16, 128), BF),
            pltpu.VMEM((16, 128), BF),
            pltpu.VMEM((TILES, 16, 128), BF),
            dma((4,)), dma((4,)),
            dma((2, 4)), dma((2, 4)),
            dma((2, 3)), dma((2, 3)),
            dma((2, 3)), dma((2, 3)),
            dma((16,)), dma((16,)),
            dma((TILES,)), dma((32,)),
            dma((15,)), dma((15,)),
            dma((31,)), dma((TILES,)),
        ],
        compiler_params=pltpu.CompilerParams(
            collective_id=0, has_side_effects=True, vmem_limit_bytes=48 * 1024 * 1024
        ),
        name="encoder_backward",
    )(
        bases, w_embed, b_embed.reshape(1, C0), gain.reshape(1, C0), taps, w_widen, cotangent
    )
    return (out[0], out[1].reshape(C0), out[2].reshape(C0), out[3], out[4])


def solution(mesh):
    return jax.shard_map(
        local,
        mesh=mesh,
        in_specs=(P("dp", "seq"), P(), P(), P(), P(), P(), P("dp", "seq", None)),
        out_specs=(P(), P(), P(), P(), P("dp", "seq")),
        check_vma=False,
    )
```

```python
import jax
import jax.numpy as jnp
from jax import lax
from jax.experimental import pallas as pl
from jax.experimental.pallas import tpu as pltpu
from jax.sharding import PartitionSpec as P

KE = 15
STEP = 64
C0 = 768
C1 = 896
BINS = 256
ROWS = BINS + 2 * STEP
TILES = 24
MESH = pl.DeviceIdType.MESH
BF = jnp.bfloat16
F32 = jnp.float32
ORDER = (2, 1, 3, 0)
PLANE = [(dc, dx, dy) for dc in range(2) for dx in range(4) for dy in range(4)][1:]
GELU_A = 0.7978845608028654
GELU_B = 0.044715


def device(x, y, z, core):
    return {"seq": (x * 8 + z % 8) * 2 + core, "dp": (z // 8) * 4 + y}


def dot(a, b, ca, cb):
    return lax.dot_general(a, b, (((ca,), (cb,)), ((), ())), preferred_element_type=F32)


def iota(shape, dim):
    return lax.broadcasted_iota(jnp.int32, shape, dim)


def chosen(shape, cond):
    return jnp.where(cond, jnp.ones(shape, F32), jnp.zeros(shape, F32)).astype(BF)


def column_choice(h, core):
    j = iota((256, 1), 0)
    a, b, i = j >> 6, (j >> 4) & 3, j & 15
    x, yq = (a, b) if h == 0 else (b, a)
    col = ((x * 8 + yq * 2 + h) * 2 + core) * 14 + i
    col = jnp.where(i < 14, col, -1)
    return chosen((256, C1), iota((256, C1), 1) == col)


def normed(pooled, gain):
    xf = pooled.astype(F32)
    rs = lax.rsqrt(jnp.mean(xf * xf, axis=-1, keepdims=True) + 1e-06)
    y = xf * rs
    n = y * gain
    t = jnp.tanh(GELU_A * (n + GELU_B * (n * n * n)))
    return rs, y, n, t


def fold(v):
    return v[0:8] + v[8:16]


def kernel(
    h_bases, h_embed, h_bias, h_gain, h_taps, h_widen, h_cot,
    agb, o_widen,
    bases, w_embed, b_embed, gain, taps, w_widen, cot,
    lb, rb, lcot, rcot, tt, paired, emb, pool, act, dblk, block, half, cot_t, sm, smb,
    own, oth, crecv, send1, recv1, acc1, send2, recv2, acc2, zsend, zrecv,
    rsrecv, part, ssend, srecv, fin, totals,
    ins, hs, hr, csem_s, csem_r, s1s, s1r, s2s, s2r, zs, zr, rss, rsr, ss, sr, gs, gr,
):
    pairs = [
        (h_bases, bases), (h_embed, w_embed), (h_bias, b_embed), (h_gain, gain),
        (h_taps, taps), (h_cot, cot), (h_widen, w_widen),
    ]
    loads = [pltpu.make_async_copy(a, b, ins.at[k]) for k, (a, b) in enumerate(pairs)]
    for c in loads:
        c.start()
    seq = lax.axis_index("seq")
    dp = lax.axis_index("dp")
    core = seq % 2
    x = seq // 16
    y = dp % 4
    z = (dp // 4) * 8 + (seq // 2) % 8
    other = 1 - core
    me = (core * 4 + x) * 4 + y
    reducer = me < TILES
    right = {"seq": (seq + 1) % 64, "dp": dp}
    left = {"seq": (seq + 63) % 64, "dp": dp}

    barrier = pltpu.get_barrier_semaphore()

    def signal(dev):
        pl.semaphore_signal(barrier, inc=1, device_id=dev, device_id_type=MESH)

    signal(right)
    signal(left)
    for dz in (8, 7, 9, 6, 10, 5, 11, 4, 12, 3, 13, 2, 14, 1, 15):
        signal(device(x, y, (z + dz) % 16, core))
    from_y = (z % 8) // 2

    @pl.when(from_y != y)
    def _():
        for k in range(16):
            signal(device(x, from_y, k, core))

    for dc, dx, dy in PLANE:
        signal(device((x + dx) % 4, (y + dy) % 4, z, (core + dc) % 2))

    def remote(src, dst, send, recv, dev):
        return pltpu.make_async_remote_copy(
            src_ref=src, dst_ref=dst, send_sem=send, recv_sem=recv,
            device_id=dev, device_id_type=MESH,
        )

    p, col = iota((C0, BINS), 0), iota((C0, BINS), 1)
    tap_of, base_of = iota((KE * 4, 16), 0) >> 2, (iota((KE * 4, BINS), 0) & 3).astype(F32)
    place = iota((KE * 4, 16), 1)
    one, zero = jnp.ones((KE * 4, BINS), F32), jnp.zeros((KE * 4, BINS), F32)

    def pairs_of(ext, bins):
        for m in range(16):
            tt[m : m + 1, :] = pltpu.roll(ext, 1024 - 121 - m, 1)
        even = chosen((C0, BINS), p == 2 * bins + 128)
        win = dot(tt[:, 0:C0].astype(BF), even, 1, 0).astype(BF)
        first = dot(chosen((KE * 4, 16), place == tap_of), win, 1, 0)
        second = dot(chosen((KE * 4, 16), place == tap_of + 1), win, 1, 0)
        return jnp.where(first == base_of, one, zero) + jnp.where(second == base_of, one, zero)

    def forward(src, dst, keep):
        v = (emb[pl.ds(src, 16)] * 0.5 + b_row).astype(BF)
        pool[pl.ds(dst, 16)] = v
        _, _, n, t = normed(v, gain_row)
        a = 0.5 * n * (1.0 + t)
        act[pl.ds(dst, 16)] = (a if keep is None else a * keep).astype(BF)

    def aligned(v):
        return pl.multiple_of(v, 16)

    def mix(i):
        total = pool[pl.ds(aligned(i * 16 + STEP), 16)].astype(F32)
        for k in (1, 0, 2):
            total = total + taps[k : k + 1] * act[pl.ds(aligned(i * 16 + k * STEP), 16)].astype(F32)
        block[pl.ds(aligned(i * 16), 16)] = total.astype(BF)

    def backward(i):
        at = [pl.ds(aligned(i * 16 + k * STEP), 16) for k in range(3)]
        d = dblk[at[1]].astype(F32)
        d_act = taps[1:2] * d
        d_act = d_act + taps[0:1] * dblk[at[2]].astype(F32)
        d_act = d_act + taps[2:3] * dblk[at[0]].astype(F32)
        rs, yv, n, t = normed(pool[at[1]], gain_row)
        slope = 0.5 * (1.0 + t) + 0.5 * n * (1.0 - t * t) * (
            GELU_A * (1.0 + 3.0 * GELU_B * (n * n))
        )
        dn = d_act * slope
        dy = dn * gain_row
        d_norm = rs * (dy - yv * jnp.mean(dy * yv, axis=-1, keepdims=True))
        half[pl.ds(aligned(i * 16), 16)] = ((d + d_norm) * 0.5).astype(BF)
        return [fold(dn * yv)] + [fold(d * act[at[k]].astype(F32)) for k in range(3)]

    for c in loads[:5]:
        c.wait()
    b_row = b_embed[...].reshape(1, C0)
    gain_row = gain[...].reshape(1, C0)
    mid = bases[...].astype(F32)
    gap = jnp.full((1, 256), -1.0, F32)
    paired[...] = pairs_of(jnp.concatenate([gap, mid, gap], axis=1), col)
    emb[...] = dot(paired[...].astype(BF), w_embed[...], 0, 0)

    def own_forward(i, _):
        for k in range(2):
            at = aligned(i * 32 + 16 * k)
            forward(at, aligned(at + STEP), None)
        return 0

    lax.fori_loop(0, BINS // 32, own_forward, 0)
    loads[5].wait()

    pl.semaphore_wait(barrier, 2 + 31 + 15 + 12)

    halo = [
        remote(bases, lb, hs.at[0], hr.at[0], right),
        remote(bases, rb, hs.at[1], hr.at[1], left),
        remote(cot.at[0, pl.ds(BINS - STEP, STEP)], lcot, hs.at[2], hr.at[2], right),
        remote(cot.at[0, pl.ds(0, STEP)], rcot, hs.at[3], hr.at[3], left),
    ]
    for c in halo:
        c.start()

    loads[6].wait()
    dblk[STEP : STEP + BINS] = dot(cot[0], w_widen[...], 1, 1).astype(BF)
    for w in range(2):
        for h in range(2):
            pick = column_choice(h, core if w == 0 else other)
            cot_t[w, h] = dot(pick, cot[0], 1, 1).astype(BF)

    totals[...] = jnp.zeros((4, 8, C0), F32)

    def add_up(news):
        for k in range(4):
            total = totals[k]
            for new in news:
                total = total + new[k]
            totals[k] = total

    def inner(i, _):
        mix(5 + 2 * i)
        mix(6 + 2 * i)
        add_up([backward(5 + 2 * i), backward(6 + 2 * i)])
        return 0

    lax.fori_loop(0, 3, inner, 0)

    halo[0].wait_recv()
    halo[1].wait_recv()
    has_left = jnp.where(seq > 0, 1.0, 0.0)
    has_right = jnp.where(seq < 63, 1.0, 0.0)
    ext = jnp.concatenate([lb[:, 256:512], bases[...], rb[:, 0:256]], axis=1)
    pos = iota((1, 1024), 1) + seq * 512 - 256
    ext = jnp.where(jnp.logical_and(pos >= 0, pos < 32768), ext, -1).astype(F32)
    bins = jnp.where(
        jnp.logical_or(col < 16, col >= 240), col, jnp.where(col < 128, col - 80, col + 128)
    )
    again = pairs_of(ext, bins)
    lane = iota((KE * 4, BINS), 1)
    paired[...] = jnp.where(jnp.logical_or(lane < 16, lane >= 240), again, paired[...])
    emb[...] = dot(again.astype(BF), w_embed[...], 0, 0)

    def rim_forward(i, _):
        forward(
            aligned(i * 16), aligned(jnp.where(i == 0, STEP, i * 16 - 16)),
            jnp.where(i == 0, 1.0, has_left),
        )
        forward(
            aligned(jnp.where(i == 4, 240, 128 + i * 16)),
            aligned(jnp.where(i == 4, STEP + 240, STEP + BINS + i * 16)),
            jnp.where(i == 4, 1.0, has_right),
        )
        return 0

    lax.fori_loop(0, 5, rim_forward, 0)

    def outer_mix(i, _):
        mix(i)
        mix(15 - i)
        return 0

    lax.fori_loop(0, 5, outer_mix, 0)

    core_copies = []
    for h in range(2):
        oth[h] = dot(cot_t[1, h], block[...], 1, 0).astype(BF).reshape(4, 4, 16, C0)
        for o in ORDER:
            tgt = (x + o) % 4 if h == 0 else (y + o) % 4
            c = remote(
                oth.at[h, tgt], crecv.at[h, o], csem_s.at[h, o], csem_r.at[h, o],
                device(x, y, z, other),
            )
            c.start()
            core_copies.append((o, h, tgt, c))
    for h in range(2):
        own[h] = dot(cot_t[0, h], block[...], 1, 0).reshape(4, 4, 16, C0)

    halo[2].wait_recv()
    halo[3].wait_recv()
    dblk[0:STEP] = (dot(lcot[...], w_widen[...], 1, 1) * has_left).astype(BF)
    dblk[STEP + BINS : ROWS] = (dot(rcot[...], w_widen[...], 1, 1) * has_right).astype(BF)

    def outer_backward(i, _):
        add_up([backward(i), backward(15 - i)])
        return 0

    lax.fori_loop(0, 5, outer_backward, 0)
    sm[0 : KE * 4] = dot(paired[...].astype(BF), half[...], 1, 0)
    for k in range(4):
        sm[KE * 4 + k : KE * 4 + k + 1] = jnp.sum(totals[k], axis=0, keepdims=True)
    for c in range(TILES):
        i, j = c // 6, c % 6
        smb[c] = sm[16 * i : 16 * i + 16, 128 * j : 128 * j + 128].astype(BF)

    rs_copies = []
    for k in range(TILES):
        c = (me + k) % TILES
        r = remote(
            smb.at[c], rsrecv.at[me], rss.at[k], rsr.at[me],
            device((c // 4) % 4, c % 4, z, c // 16),
        )
        if k == 0:
            stay = pltpu.make_async_copy(smb.at[c], rsrecv.at[me], rsr.at[me])
            pl.when(reducer)(stay.start)
            pl.when(jnp.logical_not(reducer))(r.start)
        else:
            r.start()
        rs_copies.append(r)

    copies1 = {}
    for o, h, tgt, c in core_copies:
        c.wait_recv()
        total = own[h, tgt] + crecv[h, o].astype(F32)
        if o == 0:
            acc1[h] = total
        else:
            send1[h, o - 1] = total.astype(BF)
            dev = device(tgt, y, z, core) if h == 0 else device(x, tgt, z, core)
            r = remote(
                send1.at[h, o - 1], recv1.at[h, o - 1], s1s.at[h, o - 1], s1r.at[h, o - 1], dev
            )
            r.start()
            copies1[h, o] = r

    z_small = [
        remote(
            ssend, srecv.at[dz - 1], ss.at[dz - 1], sr.at[dz - 1],
            device(x, y, (z + dz) % 16, core),
        )
        for dz in range(1, 16)
    ]

    @pl.when(reducer)
    def _():
        total = jnp.zeros((16, 128), F32)
        for k in range(32):
            remote(
                smb.at[0], rsrecv.at[k], rss.at[0], rsr.at[k], device(x, y, z, other)
            ).wait_recv()
            total = total + rsrecv[k].astype(F32)
        part[...] = total
        ssend[...] = total.astype(BF)
        for r in z_small:
            r.start()

    copies2 = {}
    for h in range(2):
        for o in (1, 3, 2):
            copies1[h, o].wait_recv()
        for o in ORDER:
            tgt = (y + o) % 4 if h == 0 else (x + o) % 4
            total = acc1[h, tgt]
            for k in range(3):
                total = total + recv1[h, k, tgt].astype(F32)
            if o == 0:
                acc2[h] = total
            else:
                send2[h, o - 1] = total.astype(BF)
                dev = device(x, tgt, z, core) if h == 0 else device(tgt, y, z, core)
                r = remote(
                    send2.at[h, o - 1], recv2.at[h, o - 1],
                    s2s.at[h, o - 1], s2r.at[h, o - 1], dev,
                )
                r.start()
                copies2[h, o] = r

    zcopies = []
    for h in range(2):
        for o in (1, 3, 2):
            copies2[h, o].wait_recv()
        total = acc2[h]
        for k in range(3):
            total = total + recv2[h, k].astype(F32)
        for d in range(8):
            piece = total[:, 96 * d : 96 * d + 96].astype(BF)
            zsend[h, d] = jnp.concatenate([piece, jnp.zeros((16, 32), BF)], axis=1)
            to_y, to_z = d % 4, (d // 4) * 8 + 2 * y + h
            r = remote(
                zsend.at[h, d], zrecv.at[z], zs.at[h * 8 + d], zr.at[z],
                device(x, to_y, to_z, core),
            )
            stay = pltpu.make_async_copy(zsend.at[h, d], zrecv.at[z], zr.at[z])
            mine = jnp.logical_and(to_y == y, to_z == z)
            pl.when(mine)(stay.start)
            pl.when(jnp.logical_not(mine))(r.start)
            zcopies.append((mine, r))

    gcopies = [
        remote(
            fin, agb.at[me], gs.at[k], gr.at[me],
            device((x + dx) % 4, (y + dy) % 4, z, (core + dc) % 2),
        )
        for k, (dc, dx, dy) in enumerate(PLANE)
    ]

    @pl.when(reducer)
    def _():
        total = part[...]
        for k in range(15):
            z_small[k].wait_recv()
            total = total + srecv[k].astype(F32)
        fin[...] = total.astype(BF)
        agb[me] = total.astype(BF)
        for r in gcopies:
            r.start()

    total = jnp.zeros((16, 128), F32)
    for k in range(16):
        remote(
            zsend.at[0, 0], zrecv.at[k], zs.at[0], zr.at[k], device(x, y, z, other)
        ).wait_recv()
        total = total + zrecv[k].astype(F32)
    o_widen[...] = total

    for c in range(TILES):
        r = remote(fin, agb.at[c], gs.at[0], gr.at[c], device(x, y, z, other))
        pl.when(me != c)(r.wait_recv)
    for c in halo:
        c.wait_send()
    for _, _, _, c in core_copies:
        c.wait_send()
    for c in list(copies1.values()) + list(copies2.values()) + rs_copies[1:]:
        c.wait_send()
    pl.when(jnp.logical_not(reducer))(rs_copies[0].wait_send)

    @pl.when(reducer)
    def _():
        for r in z_small + gcopies:
            r.wait_send()

    for mine, r in zcopies:
        pl.when(jnp.logical_not(mine))(r.wait_send)


def finish(agb, wid, o_embed, o_bias, o_gain, o_taps, o_widen):
    rows = []
    for i in range(4):
        rows.append(jnp.concatenate([agb[6 * i + j] for j in range(6)], axis=1).astype(F32))
    o_embed[0:48] = jnp.concatenate(rows[:3], axis=0)
    o_embed[48:60] = rows[3][0:12]
    o_bias[...] = jnp.sum(rows[1][12:16], axis=0, keepdims=True).reshape(C0)
    o_gain[...] = rows[3][12:13].reshape(C0)
    o_taps[...] = rows[3][13:16]
    o_widen[...] = wid[...].T[0:96, 0:14]


def local(bases, w_embed, b_embed, gain, taps, w_widen, cotangent):
    dma = pltpu.SemaphoreType.DMA
    vmem = pl.BlockSpec(memory_space=pltpu.VMEM)
    agb, wid = pl.pallas_call(
        kernel,
        out_shape=(
            jax.ShapeDtypeStruct((TILES, 16, 128), BF),
            jax.ShapeDtypeStruct((16, 128), F32),
        ),
        in_specs=[pl.BlockSpec(memory_space=pltpu.HBM)] * 7,
        out_specs=(vmem,) * 2,
        scratch_shapes=[
            pltpu.VMEM((1, 512), jnp.int32),
            pltpu.VMEM((KE * 4, C0), BF),
            pltpu.VMEM((C0,), F32),
            pltpu.VMEM((C0,), F32),
            pltpu.VMEM((3, C0), F32),
            pltpu.VMEM((C0, C1), BF),
            pltpu.VMEM((1, BINS, C1), BF),
            pltpu.VMEM((1, 512), jnp.int32),
            pltpu.VMEM((1, 512), jnp.int32),
            pltpu.VMEM((STEP, C1), BF),
            pltpu.VMEM((STEP, C1), BF),
            pltpu.VMEM((16, 1024), F32),
            pltpu.VMEM((KE * 4, BINS), F32),
            pltpu.VMEM((BINS, C0), F32),
            pltpu.VMEM((ROWS, C0), BF),
            pltpu.VMEM((ROWS, C0), BF),
            pltpu.VMEM((ROWS, C0), BF),
            pltpu.VMEM((BINS, C0), BF),
            pltpu.VMEM((BINS, C0), BF),
            pltpu.VMEM((2, 2, 256, BINS), BF),
            pltpu.VMEM((64, C0), F32),
            pltpu.VMEM((TILES, 16, 128), BF),
            pltpu.VMEM((2, 4, 4, 16, C0), F32),
            pltpu.VMEM((2, 4, 4, 16, C0), BF),
            pltpu.VMEM((2, 4, 4, 16, C0), BF),
            pltpu.VMEM((2, 3, 4, 16, C0), BF),
            pltpu.VMEM((2, 3, 4, 16, C0), BF),
            pltpu.VMEM((2, 4, 16, C0), F32),
            pltpu.VMEM((2, 3, 16, C0), BF),
            pltpu.VMEM((2, 3, 16, C0), BF),
            pltpu.VMEM((2, 16, C0), F32),
            pltpu.VMEM((2, 8, 16, 128), BF),
            pltpu.VMEM((16, 16, 128), BF),
            pltpu.VMEM((32, 16, 128), BF),
            pltpu.VMEM((16, 128), F32),
            pltpu.VMEM((16, 128), BF),
            pltpu.VMEM((15, 16, 128), BF),
            pltpu.VMEM((16, 128), BF),
            pltpu.VMEM((4, 8, C0), F32),
            dma((7,)),
            dma((4,)), dma((4,)),
            dma((2, 4)), dma((2, 4)),
            dma((2, 3)), dma((2, 3)),
            dma((2, 3)), dma((2, 3)),
            dma((16,)), dma((16,)),
            dma((TILES,)), dma((32,)),
            dma((15,)), dma((15,)),
            dma((31,)), dma((TILES,)),
        ],
        compiler_params=pltpu.CompilerParams(
            collective_id=0, has_side_effects=True, vmem_limit_bytes=48 * 1024 * 1024
        ),
        name="encoder_backward",
    )(bases, w_embed, b_embed, gain, taps, w_widen, cotangent)
    out = pl.pallas_call(
        finish,
        out_shape=(
            jax.ShapeDtypeStruct((KE * 4, C0), F32),
            jax.ShapeDtypeStruct((C0,), F32),
            jax.ShapeDtypeStruct((C0,), F32),
            jax.ShapeDtypeStruct((3, C0), F32),
            jax.ShapeDtypeStruct((96, 14), F32),
        ),
        in_specs=[vmem] * 2,
        out_specs=(vmem,) * 5,
        name="finish",
    )(agb, wid)
    return tuple(out)


def solution(mesh):
    return jax.shard_map(
        local,
        mesh=mesh,
        in_specs=(P("dp", "seq"), P(), P(), P(), P(), P(), P("dp", "seq", None)),
        out_specs=(P(), P(), P(), P(), P("dp", "seq")),
        check_vma=False,
    )
```

```python
import jax
import jax.numpy as jnp
from jax import lax
from jax.experimental import pallas as pl
from jax.experimental.pallas import tpu as pltpu
from jax.sharding import PartitionSpec as P

KE = 15
STEP = 64
C0 = 768
C1 = 896
BINS = 256
ROWS = BINS + 2 * STEP
TILES = 24
MESH = pl.DeviceIdType.MESH
BF = jnp.bfloat16
F32 = jnp.float32
ORDER = (2, 1, 3, 0)
PLANE = [(dc, dx, dy) for dc in range(2) for dx in range(4) for dy in range(4)][1:]
GELU_A = 0.7978845608028654
GELU_B = 0.044715


def device(x, y, z, core):
    return {"seq": (x * 8 + z % 8) * 2 + core, "dp": (z // 8) * 4 + y}


def dot(a, b, ca, cb):
    return lax.dot_general(a, b, (((ca,), (cb,)), ((), ())), preferred_element_type=F32)


def iota(shape, dim):
    return lax.broadcasted_iota(jnp.int32, shape, dim)


def chosen(shape, cond):
    return jnp.where(cond, jnp.ones(shape, F32), jnp.zeros(shape, F32)).astype(BF)


def column_choice(h, core):
    j = iota((256, 1), 0)
    a, b, i = j >> 6, (j >> 4) & 3, j & 15
    x, yq = (a, b) if h == 0 else (b, a)
    col = ((x * 8 + yq * 2 + h) * 2 + core) * 14 + i
    col = jnp.where(i < 14, col, -1)
    return chosen((256, C1), iota((256, C1), 1) == col)


def normed(pooled, gain):
    xf = pooled.astype(F32)
    rs = lax.rsqrt(jnp.mean(xf * xf, axis=-1, keepdims=True) + 1e-06)
    y = xf * rs
    n = y * gain
    t = jnp.tanh(GELU_A * (n + GELU_B * (n * n * n)))
    return rs, y, n, t


def fold(v):
    return v[0:8] + v[8:16]


def kernel(
    h_bases, h_embed, h_bias, h_gain, h_taps, h_widen, h_cot,
    agb, o_widen,
    bases, w_embed, b_embed, gain, taps, w_widen, cot,
    lb, rb, lcot, rcot, tt, paired, emb, pool, act, dblk, block, half, cot_t, sm, smb,
    own, oth, crecv, send1, recv1, acc1, send2, recv2, acc2, zsend, zrecv,
    rsrecv, part, ssend, srecv, fin, totals,
    ins, hs, hr, csem_s, csem_r, s1s, s1r, s2s, s2r, zs, zr, rss, rsr, ss, sr, gs, gr,
):
    pairs = [
        (h_bases, bases), (h_embed, w_embed), (h_bias, b_embed), (h_gain, gain),
        (h_taps, taps), (h_cot, cot), (h_widen, w_widen),
    ]
    loads = [pltpu.make_async_copy(a, b, ins.at[k]) for k, (a, b) in enumerate(pairs)]
    for c in loads:
        c.start()
    seq = lax.axis_index("seq")
    dp = lax.axis_index("dp")
    core = seq % 2
    x = seq // 16
    y = dp % 4
    z = (dp // 4) * 8 + (seq // 2) % 8
    other = 1 - core
    me = (core * 4 + x) * 4 + y
    reducer = me < TILES
    right = {"seq": (seq + 1) % 64, "dp": dp}
    left = {"seq": (seq + 63) % 64, "dp": dp}

    barrier = pltpu.get_barrier_semaphore()

    def signal(dev):
        pl.semaphore_signal(barrier, inc=1, device_id=dev, device_id_type=MESH)

    signal(right)
    signal(left)
    for dz in (8, 7, 9, 6, 10, 5, 11, 4, 12, 3, 13, 2, 14, 1, 15):
        signal(device(x, y, (z + dz) % 16, core))
    from_y = (z % 8) // 2

    @pl.when(from_y != y)
    def _():
        for k in range(16):
            signal(device(x, from_y, k, core))

    for dc, dx, dy in PLANE:
        signal(device((x + dx) % 4, (y + dy) % 4, z, (core + dc) % 2))

    def remote(src, dst, send, recv, dev):
        return pltpu.make_async_remote_copy(
            src_ref=src, dst_ref=dst, send_sem=send, recv_sem=recv,
            device_id=dev, device_id_type=MESH,
        )

    p, col = iota((C0, BINS), 0), iota((C0, BINS), 1)
    tap_of, base_of = iota((KE * 4, 16), 0) >> 2, (iota((KE * 4, BINS), 0) & 3).astype(F32)
    place = iota((KE * 4, 16), 1)
    one, zero = jnp.ones((KE * 4, BINS), F32), jnp.zeros((KE * 4, BINS), F32)

    def pairs_of(ext, bins):
        for m in range(16):
            tt[m : m + 1, :] = pltpu.roll(ext, 1024 - 121 - m, 1)
        even = chosen((C0, BINS), p == 2 * bins + 128)
        win = dot(tt[:, 0:C0].astype(BF), even, 1, 0).astype(BF)
        first = dot(chosen((KE * 4, 16), place == tap_of), win, 1, 0)
        second = dot(chosen((KE * 4, 16), place == tap_of + 1), win, 1, 0)
        return jnp.where(first == base_of, one, zero) + jnp.where(second == base_of, one, zero)

    def forward(src, dst, keep):
        v = (emb[pl.ds(src, 16)] * 0.5 + b_row).astype(BF)
        pool[pl.ds(dst, 16)] = v
        _, _, n, t = normed(v, gain_row)
        a = 0.5 * n * (1.0 + t)
        act[pl.ds(dst, 16)] = (a if keep is None else a * keep).astype(BF)

    def aligned(v):
        return pl.multiple_of(v, 16)

    def mix(i):
        total = pool[pl.ds(aligned(i * 16 + STEP), 16)].astype(F32)
        for k in (1, 0, 2):
            total = total + taps[k : k + 1] * act[pl.ds(aligned(i * 16 + k * STEP), 16)].astype(F32)
        block[pl.ds(aligned(i * 16), 16)] = total.astype(BF)

    def backward(i):
        at = [pl.ds(aligned(i * 16 + k * STEP), 16) for k in range(3)]
        d = dblk[at[1]].astype(F32)
        d_act = taps[1:2] * d
        d_act = d_act + taps[0:1] * dblk[at[2]].astype(F32)
        d_act = d_act + taps[2:3] * dblk[at[0]].astype(F32)
        rs, yv, n, t = normed(pool[at[1]], gain_row)
        slope = 0.5 * (1.0 + t) + 0.5 * n * (1.0 - t * t) * (
            GELU_A * (1.0 + 3.0 * GELU_B * (n * n))
        )
        dn = d_act * slope
        dy = dn * gain_row
        d_norm = rs * (dy - yv * jnp.mean(dy * yv, axis=-1, keepdims=True))
        half[pl.ds(aligned(i * 16), 16)] = ((d + d_norm) * 0.5).astype(BF)
        return [fold(dn * yv)] + [fold(d * act[at[k]].astype(F32)) for k in range(3)]

    for c in loads[:5]:
        c.wait()
    b_row = b_embed[...].reshape(1, C0)
    gain_row = gain[...].reshape(1, C0)
    mid = bases[...].astype(F32)
    gap = jnp.full((1, 256), -1.0, F32)
    paired[...] = pairs_of(jnp.concatenate([gap, mid, gap], axis=1), col)
    emb[...] = dot(paired[...].astype(BF), w_embed[...], 0, 0)

    def own_forward(i, _):
        for k in range(2):
            at = aligned(i * 32 + 16 * k)
            forward(at, aligned(at + STEP), None)
        return 0

    lax.fori_loop(0, BINS // 32, own_forward, 0)
    loads[5].wait()

    pl.semaphore_wait(barrier, 2 + 31 + 15 + 12)

    halo = [
        remote(bases, lb, hs.at[0], hr.at[0], right),
        remote(bases, rb, hs.at[1], hr.at[1], left),
        remote(cot.at[0, pl.ds(BINS - STEP, STEP)], lcot, hs.at[2], hr.at[2], right),
        remote(cot.at[0, pl.ds(0, STEP)], rcot, hs.at[3], hr.at[3], left),
    ]
    for c in halo:
        c.start()

    loads[6].wait()
    dblk[STEP : STEP + BINS] = dot(cot[0], w_widen[...], 1, 1).astype(BF)
    for w in range(2):
        for h in range(2):
            pick = column_choice(h, core if w == 0 else other)
            cot_t[w, h] = dot(pick, cot[0], 1, 1).astype(BF)

    totals[...] = jnp.zeros((4, 8, C0), F32)

    def add_up(news):
        for k in range(4):
            total = totals[k]
            for new in news:
                total = total + new[k]
            totals[k] = total

    def inner(i, _):
        mix(5 + 2 * i)
        mix(6 + 2 * i)
        add_up([backward(5 + 2 * i), backward(6 + 2 * i)])
        return 0

    lax.fori_loop(0, 3, inner, 0)

    halo[0].wait_recv()
    halo[1].wait_recv()
    has_left = jnp.where(seq > 0, 1.0, 0.0)
    has_right = jnp.where(seq < 63, 1.0, 0.0)
    ext = jnp.concatenate([lb[:, 256:512], bases[...], rb[:, 0:256]], axis=1)
    pos = iota((1, 1024), 1) + seq * 512 - 256
    ext = jnp.where(jnp.logical_and(pos >= 0, pos < 32768), ext, -1).astype(F32)
    bins = jnp.where(
        jnp.logical_or(col < 16, col >= 240), col, jnp.where(col < 128, col - 80, col + 128)
    )
    again = pairs_of(ext, bins)
    lane = iota((KE * 4, BINS), 1)
    paired[...] = jnp.where(jnp.logical_or(lane < 16, lane >= 240), again, paired[...])
    emb[...] = dot(again.astype(BF), w_embed[...], 0, 0)

    def rim_forward(i, _):
        forward(
            aligned(i * 16), aligned(jnp.where(i == 0, STEP, i * 16 - 16)),
            jnp.where(i == 0, 1.0, has_left),
        )
        forward(
            aligned(jnp.where(i == 4, 240, 128 + i * 16)),
            aligned(jnp.where(i == 4, STEP + 240, STEP + BINS + i * 16)),
            jnp.where(i == 4, 1.0, has_right),
        )
        return 0

    lax.fori_loop(0, 5, rim_forward, 0)

    def outer_mix(i, _):
        mix(i)
        mix(15 - i)
        return 0

    lax.fori_loop(0, 5, outer_mix, 0)

    core_copies = []
    for h in range(2):
        oth[h] = dot(cot_t[1, h], block[...], 1, 0).astype(BF).reshape(4, 4, 16, C0)
        for o in ORDER:
            tgt = (x + o) % 4 if h == 0 else (y + o) % 4
            c = remote(
                oth.at[h, tgt], crecv.at[h, o], csem_s.at[h, o], csem_r.at[h, o],
                device(x, y, z, other),
            )
            c.start()
            core_copies.append((o, h, tgt, c))
    for h in range(2):
        own[h] = dot(cot_t[0, h], block[...], 1, 0).reshape(4, 4, 16, C0)

    halo[2].wait_recv()
    halo[3].wait_recv()
    dblk[0:STEP] = (dot(lcot[...], w_widen[...], 1, 1) * has_left).astype(BF)
    dblk[STEP + BINS : ROWS] = (dot(rcot[...], w_widen[...], 1, 1) * has_right).astype(BF)

    def outer_backward(i, _):
        add_up([backward(i), backward(15 - i)])
        return 0

    lax.fori_loop(0, 5, outer_backward, 0)
    sm[0 : KE * 4] = dot(paired[...].astype(BF), half[...], 1, 0)
    for k in range(4):
        sm[KE * 4 + k : KE * 4 + k + 1] = jnp.sum(totals[k], axis=0, keepdims=True)
    for c in range(TILES):
        i, j = c // 6, c % 6
        smb[c] = sm[16 * i : 16 * i + 16, 128 * j : 128 * j + 128].astype(BF)

    rs_copies = []
    for k in range(TILES):
        c = (me + k) % TILES
        r = remote(
            smb.at[c], rsrecv.at[me], rss.at[k], rsr.at[me],
            device((c // 4) % 4, c % 4, z, c // 16),
        )
        if k == 0:
            stay = pltpu.make_async_copy(smb.at[c], rsrecv.at[me], rsr.at[me])
            pl.when(reducer)(stay.start)
            pl.when(jnp.logical_not(reducer))(r.start)
        else:
            r.start()
        rs_copies.append(r)

    copies1 = {}
    for o, h, tgt, c in core_copies:
        c.wait_recv()
        total = own[h, tgt] + crecv[h, o].astype(F32)
        if o == 0:
            acc1[h] = total
        else:
            send1[h, o - 1] = total.astype(BF)
            dev = device(tgt, y, z, core) if h == 0 else device(x, tgt, z, core)
            r = remote(
                send1.at[h, o - 1], recv1.at[h, o - 1], s1s.at[h, o - 1], s1r.at[h, o - 1], dev
            )
            r.start()
            copies1[h, o] = r

    z_small = [
        remote(
            ssend, srecv.at[dz - 1], ss.at[dz - 1], sr.at[dz - 1],
            device(x, y, (z + dz) % 16, core),
        )
        for dz in range(1, 16)
    ]

    @pl.when(reducer)
    def _():
        total = jnp.zeros((16, 128), F32)
        for k in range(32):
            remote(
                smb.at[0], rsrecv.at[k], rss.at[0], rsr.at[k], device(x, y, z, other)
            ).wait_recv()
            total = total + rsrecv[k].astype(F32)
        part[...] = total
        ssend[...] = total.astype(BF)
        for r in z_small:
            r.start()

    copies2 = {}
    for h in range(2):
        for o in (1, 3, 2):
            copies1[h, o].wait_recv()
        for o in ORDER:
            tgt = (y + o) % 4 if h == 0 else (x + o) % 4
            total = acc1[h, tgt]
            for k in range(3):
                total = total + recv1[h, k, tgt].astype(F32)
            if o == 0:
                acc2[h] = total
            else:
                send2[h, o - 1] = total.astype(BF)
                dev = device(x, tgt, z, core) if h == 0 else device(tgt, y, z, core)
                r = remote(
                    send2.at[h, o - 1], recv2.at[h, o - 1],
                    s2s.at[h, o - 1], s2r.at[h, o - 1], dev,
                )
                r.start()
                copies2[h, o] = r

    zcopies = []
    for h in range(2):
        for o in (1, 3, 2):
            copies2[h, o].wait_recv()
        total = acc2[h]
        for k in range(3):
            total = total + recv2[h, k].astype(F32)
        for d in range(8):
            piece = total[:, 96 * d : 96 * d + 96].astype(BF)
            zsend[h, d] = jnp.concatenate([piece, jnp.zeros((16, 32), BF)], axis=1)
            to_y, to_z = d % 4, (d // 4) * 8 + 2 * y + h
            r = remote(
                zsend.at[h, d], zrecv.at[z], zs.at[h * 8 + d], zr.at[z],
                device(x, to_y, to_z, core),
            )
            stay = pltpu.make_async_copy(zsend.at[h, d], zrecv.at[z], zr.at[z])
            mine = jnp.logical_and(to_y == y, to_z == z)
            pl.when(mine)(stay.start)
            pl.when(jnp.logical_not(mine))(r.start)
            zcopies.append((mine, r))

    gcopies = [
        remote(
            fin, agb.at[me], gs.at[k], gr.at[me],
            device((x + dx) % 4, (y + dy) % 4, z, (core + dc) % 2),
        )
        for k, (dc, dx, dy) in enumerate(PLANE)
    ]

    @pl.when(reducer)
    def _():
        total = part[...]
        for k in range(15):
            z_small[k].wait_recv()
            total = total + srecv[k].astype(F32)
        fin[...] = total.astype(BF)
        agb[me] = total.astype(BF)
        for r in gcopies:
            r.start()

    total = jnp.zeros((16, 128), F32)
    for k in range(16):
        remote(
            zsend.at[0, 0], zrecv.at[k], zs.at[0], zr.at[k], device(x, y, z, other)
        ).wait_recv()
        total = total + zrecv[k].astype(F32)
    o_widen[...] = total

    for c in range(TILES):
        r = remote(fin, agb.at[c], gs.at[0], gr.at[c], device(x, y, z, other))
        pl.when(me != c)(r.wait_recv)
    for c in halo:
        c.wait_send()
    for _, _, _, c in core_copies:
        c.wait_send()
    for c in list(copies1.values()) + list(copies2.values()) + rs_copies[1:]:
        c.wait_send()
    pl.when(jnp.logical_not(reducer))(rs_copies[0].wait_send)

    @pl.when(reducer)
    def _():
        for r in z_small + gcopies:
            r.wait_send()

    for mine, r in zcopies:
        pl.when(jnp.logical_not(mine))(r.wait_send)


def finish(agb, wid, o_embed, o_bias, o_gain, o_taps, o_widen):
    rows = []
    for i in range(4):
        rows.append(jnp.concatenate([agb[6 * i + j] for j in range(6)], axis=1).astype(F32))
    o_embed[0:48] = jnp.concatenate(rows[:3], axis=0)
    o_embed[48:60] = rows[3][0:12]
    o_bias[...] = jnp.sum(rows[1][12:16], axis=0, keepdims=True).reshape(C0)
    o_gain[...] = rows[3][12:13].reshape(C0)
    o_taps[...] = rows[3][13:16]
    o_widen[...] = wid[0:14, 0:96]


def local(bases, w_embed, b_embed, gain, taps, w_widen, cotangent):
    dma = pltpu.SemaphoreType.DMA
    vmem = pl.BlockSpec(memory_space=pltpu.VMEM)
    agb, wid = pl.pallas_call(
        kernel,
        out_shape=(
            jax.ShapeDtypeStruct((TILES, 16, 128), BF),
            jax.ShapeDtypeStruct((16, 128), F32),
        ),
        in_specs=[pl.BlockSpec(memory_space=pltpu.HBM)] * 7,
        out_specs=(vmem,) * 2,
        scratch_shapes=[
            pltpu.VMEM((1, 512), jnp.int32),
            pltpu.VMEM((KE * 4, C0), BF),
            pltpu.VMEM((C0,), F32),
            pltpu.VMEM((C0,), F32),
            pltpu.VMEM((3, C0), F32),
            pltpu.VMEM((C0, C1), BF),
            pltpu.VMEM((1, BINS, C1), BF),
            pltpu.VMEM((1, 512), jnp.int32),
            pltpu.VMEM((1, 512), jnp.int32),
            pltpu.VMEM((STEP, C1), BF),
            pltpu.VMEM((STEP, C1), BF),
            pltpu.VMEM((16, 1024), F32),
            pltpu.VMEM((KE * 4, BINS), F32),
            pltpu.VMEM((BINS, C0), F32),
            pltpu.VMEM((ROWS, C0), BF),
            pltpu.VMEM((ROWS, C0), BF),
            pltpu.VMEM((ROWS, C0), BF),
            pltpu.VMEM((BINS, C0), BF),
            pltpu.VMEM((BINS, C0), BF),
            pltpu.VMEM((2, 2, 256, BINS), BF),
            pltpu.VMEM((64, C0), F32),
            pltpu.VMEM((TILES, 16, 128), BF),
            pltpu.VMEM((2, 4, 4, 16, C0), F32),
            pltpu.VMEM((2, 4, 4, 16, C0), BF),
            pltpu.VMEM((2, 4, 4, 16, C0), BF),
            pltpu.VMEM((2, 3, 4, 16, C0), BF),
            pltpu.VMEM((2, 3, 4, 16, C0), BF),
            pltpu.VMEM((2, 4, 16, C0), F32),
            pltpu.VMEM((2, 3, 16, C0), BF),
            pltpu.VMEM((2, 3, 16, C0), BF),
            pltpu.VMEM((2, 16, C0), F32),
            pltpu.VMEM((2, 8, 16, 128), BF),
            pltpu.VMEM((16, 16, 128), BF),
            pltpu.VMEM((32, 16, 128), BF),
            pltpu.VMEM((16, 128), F32),
            pltpu.VMEM((16, 128), BF),
            pltpu.VMEM((15, 16, 128), BF),
            pltpu.VMEM((16, 128), BF),
            pltpu.VMEM((4, 8, C0), F32),
            dma((7,)),
            dma((4,)), dma((4,)),
            dma((2, 4)), dma((2, 4)),
            dma((2, 3)), dma((2, 3)),
            dma((2, 3)), dma((2, 3)),
            dma((16,)), dma((16,)),
            dma((TILES,)), dma((32,)),
            dma((15,)), dma((15,)),
            dma((31,)), dma((TILES,)),
        ],
        compiler_params=pltpu.CompilerParams(
            collective_id=0, has_side_effects=True, vmem_limit_bytes=60 * 1024 * 1024
        ),
        name="encoder_backward",
    )(bases, w_embed, b_embed, gain, taps, w_widen, cotangent)
    out = pl.pallas_call(
        finish,
        out_shape=(
            jax.ShapeDtypeStruct((KE * 4, C0), F32),
            jax.ShapeDtypeStruct((C0,), F32),
            jax.ShapeDtypeStruct((C0,), F32),
            jax.ShapeDtypeStruct((3, C0), F32),
            jax.ShapeDtypeStruct((14, 96), F32),
        ),
        in_specs=[vmem] * 2,
        out_specs=(vmem,) * 5,
        compiler_params=pltpu.CompilerParams(vmem_limit_bytes=60 * 1024 * 1024),
        name="finish",
    )(agb, wid)
    return (*out[:4], out[4].T)


def solution(mesh):
    return jax.shard_map(
        local,
        mesh=mesh,
        in_specs=(P("dp", "seq"), P(), P(), P(), P(), P(), P("dp", "seq", None)),
        out_specs=(P(), P(), P(), P(), P("dp", "seq")),
        check_vma=False,
    )
```

```python
import jax
import jax.numpy as jnp
from jax import lax
from jax.experimental import pallas as pl
from jax.experimental.pallas import tpu as pltpu
from jax.sharding import PartitionSpec as P

KE = 15
STEP = 64
C0 = 768
C1 = 896
BINS = 256
ROWS = BINS + 2 * STEP
TILES = 24
MESH = pl.DeviceIdType.MESH
BF = jnp.bfloat16
F32 = jnp.float32
ORDER = (2, 1, 3, 0)
PLANE = [(dc, dx, dy) for dx in (2, 1, 3, 0) for dy in (2, 1, 3, 0) for dc in (1, 0)][:-1]
NEAR = (4, 12, 3, 13, 2, 14, 1, 15)
GELU_A = 0.7978845608028654
GELU_B = 0.044715


def device(x, y, z, core):
    return {"seq": (x * 8 + z % 8) * 2 + core, "dp": (z // 8) * 4 + y}


def dot(a, b, ca, cb):
    return lax.dot_general(a, b, (((ca,), (cb,)), ((), ())), preferred_element_type=F32)


def iota(shape, dim):
    return lax.broadcasted_iota(jnp.int32, shape, dim)


def chosen(shape, cond):
    return jnp.where(cond, jnp.ones(shape, F32), jnp.zeros(shape, F32)).astype(BF)


def column_choice(h, core):
    j = iota((256, 1), 0)
    a, b, i = j >> 6, (j >> 4) & 3, j & 15
    x, yq = (a, b) if h == 0 else (b, a)
    col = ((x * 8 + yq * 2 + h) * 2 + core) * 14 + i
    col = jnp.where(i < 14, col, -1)
    return chosen((256, C1), iota((256, C1), 1) == col)


def normed(pooled, gain):
    xf = pooled.astype(F32)
    rs = lax.rsqrt(jnp.mean(xf * xf, axis=-1, keepdims=True) + 1e-06)
    y = xf * rs
    n = y * gain
    t = jnp.tanh(GELU_A * (n + GELU_B * (n * n * n)))
    return rs, y, n, t


def fold(v):
    return v[0:8] + v[8:16]


def kernel(
    h_bases, h_embed, h_bias, h_gain, h_taps, h_widen, h_cot,
    agb, o_widen,
    bases, w_embed, b_embed, gain, taps, w_widen, cot,
    lb, rb, rim, tt, paired, emb, pool, act, dblk, block, half, cot_t, sm, smb,
    own, oth, crecv, send1, recv1, acc1, send2, recv2, acc2, zsend, zrecv,
    rsrecv, part, ssend, srecv, fin, totals,
    ins, heard, hs, hr, csem_s, csem_r, s1s, s1r, s2s, s2r, zs, zr, rss, rsr, ss, sr, gs, gr,
):
    pairs = [
        (h_bases, bases), (h_embed, w_embed), (h_bias, b_embed), (h_gain, gain),
        (h_taps, taps), (h_cot, cot), (h_widen, w_widen),
    ]
    loads = [pltpu.make_async_copy(a, b, ins.at[k]) for k, (a, b) in enumerate(pairs)]
    for c in loads:
        c.start()
    seq = lax.axis_index("seq")
    dp = lax.axis_index("dp")
    core = seq % 2
    x = seq // 16
    y = dp % 4
    z = (dp // 4) * 8 + (seq // 2) % 8
    other = 1 - core
    me = (core * 4 + x) * 4 + y
    reducer = me < TILES
    right = {"seq": (seq + 1) % 64, "dp": dp}
    left = {"seq": (seq + 63) % 64, "dp": dp}

    barrier = pltpu.get_barrier_semaphore()

    def signal(sem, dev):
        pl.semaphore_signal(sem, inc=1, device_id=dev, device_id_type=MESH)

    signal(barrier, right)
    signal(barrier, left)
    for dz in NEAR:
        signal(barrier, device(x, y, (z + dz) % 16, core))
    for dc, dx, dy in PLANE:
        signal(barrier, device((x + dx) % 4, (y + dy) % 4, z, (core + dc) % 2))

    def remote(src, dst, send, recv, dev):
        return pltpu.make_async_remote_copy(
            src_ref=src, dst_ref=dst, send_sem=send, recv_sem=recv,
            device_id=dev, device_id_type=MESH,
        )

    p, col = iota((C0, BINS), 0), iota((C0, BINS), 1)
    tap_of, base_of = iota((KE * 4, 16), 0) >> 2, (iota((KE * 4, BINS), 0) & 3).astype(F32)
    place = iota((KE * 4, 16), 1)
    one, zero = jnp.ones((KE * 4, BINS), F32), jnp.zeros((KE * 4, BINS), F32)

    def pairs_of(ext, bins):
        for m in range(16):
            tt[m : m + 1, :] = pltpu.roll(ext, 1024 - 121 - m, 1)
        even = chosen((C0, BINS), p == 2 * bins + 128)
        win = dot(tt[:, 0:C0].astype(BF), even, 1, 0).astype(BF)
        first = dot(chosen((KE * 4, 16), place == tap_of), win, 1, 0)
        second = dot(chosen((KE * 4, 16), place == tap_of + 1), win, 1, 0)
        return jnp.where(first == base_of, one, zero) + jnp.where(second == base_of, one, zero)

    def forward(src, dst, keep):
        v = (emb[pl.ds(src, 16)] * 0.5 + b_row).astype(BF)
        pool[pl.ds(dst, 16)] = v
        _, _, n, t = normed(v, gain_row)
        a = 0.5 * n * (1.0 + t)
        act[pl.ds(dst, 16)] = (a if keep is None else a * keep).astype(BF)

    def aligned(v):
        return v if isinstance(v, int) else pl.multiple_of(v, 16)

    def mix(i):
        total = pool[pl.ds(aligned(i * 16 + STEP), 16)].astype(F32)
        for k in (1, 0, 2):
            total = total + taps[k : k + 1] * act[pl.ds(aligned(i * 16 + k * STEP), 16)].astype(F32)
        block[pl.ds(aligned(i * 16), 16)] = total.astype(BF)

    def backward(i):
        at = [pl.ds(aligned(i * 16 + k * STEP), 16) for k in range(3)]
        d = dblk[at[1]].astype(F32)
        d_act = taps[1:2] * d
        d_act = d_act + taps[0:1] * dblk[at[2]].astype(F32)
        d_act = d_act + taps[2:3] * dblk[at[0]].astype(F32)
        rs, yv, n, t = normed(pool[at[1]], gain_row)
        slope = 0.5 * (1.0 + t) + 0.5 * n * (1.0 - t * t) * (
            GELU_A * (1.0 + 3.0 * GELU_B * (n * n))
        )
        dn = d_act * slope
        dy = dn * gain_row
        d_norm = rs * (dy - yv * jnp.mean(dy * yv, axis=-1, keepdims=True))
        half[pl.ds(aligned(i * 16), 16)] = ((d + d_norm) * 0.5).astype(BF)
        return [fold(dn * yv)] + [fold(d * act[at[k]].astype(F32)) for k in range(3)]

    for c in loads[:5]:
        c.wait()
    b_row = b_embed[...].reshape(1, C0)
    gain_row = gain[...].reshape(1, C0)
    mid = bases[...].astype(F32)
    gap = jnp.full((1, 256), -1.0, F32)
    paired[...] = pairs_of(jnp.concatenate([gap, mid, gap], axis=1), col)
    emb[...] = dot(paired[...].astype(BF), w_embed[...], 0, 0)

    def own_forward(i, _):
        for k in range(2):
            at = aligned(i * 32 + 16 * k)
            forward(at, aligned(at + STEP), None)
        return 0

    lax.fori_loop(0, BINS // 32, own_forward, 0)
    loads[5].wait()

    pl.semaphore_wait(barrier, 2 + len(NEAR) + len(PLANE))

    halo = [
        remote(bases, lb, hs.at[0], hr.at[0], right),
        remote(bases, rb, hs.at[1], hr.at[1], left),
        remote(cot.at[0, pl.ds(BINS - STEP, STEP)], rim.at[pl.ds(0, STEP)], hs.at[2], hr.at[2], right),
        remote(cot.at[0, pl.ds(0, STEP)], rim.at[pl.ds(STEP, STEP)], hs.at[3], hr.at[3], left),
    ]
    for c in halo:
        c.start()
    for dz in NEAR:
        signal(heard.at[0], device(x, y, (z + dz) % 16, core))

    loads[6].wait()
    dblk[STEP : STEP + BINS] = dot(cot[0], w_widen[...], 1, 1).astype(BF)
    for w in range(2):
        for h in range(2):
            pick = column_choice(h, core if w == 0 else other)
            cot_t[w, h] = dot(pick, cot[0], 1, 1).astype(BF)

    totals[...] = jnp.zeros((4, 8, C0), F32)

    def add_up(news):
        for k in range(4):
            total = totals[k]
            for new in news:
                total = total + new[k]
            totals[k] = total

    def inner(i, _):
        mix(5 + 2 * i)
        mix(6 + 2 * i)
        add_up([backward(5 + 2 * i), backward(6 + 2 * i)])
        return 0

    lax.fori_loop(0, 3, inner, 0)

    pl.semaphore_wait(heard.at[0], len(NEAR))
    for dz in NEAR:
        signal(heard.at[1], device(x, y, (z + dz) % 16, core))

    halo[0].wait_recv()
    halo[1].wait_recv()
    has_left = jnp.where(seq > 0, 1.0, 0.0)
    has_right = jnp.where(seq < 63, 1.0, 0.0)
    ext = jnp.concatenate([lb[:, 256:512], bases[...], rb[:, 0:256]], axis=1)
    pos = iota((1, 1024), 1) + seq * 512 - 256
    ext = jnp.where(jnp.logical_and(pos >= 0, pos < 32768), ext, -1).astype(F32)
    bins = jnp.where(
        jnp.logical_or(col < 16, col >= 240), col, jnp.where(col < 128, col - 80, col + 128)
    )
    again = pairs_of(ext, bins)
    lane = iota((KE * 4, BINS), 1)
    paired[...] = jnp.where(jnp.logical_or(lane < 16, lane >= 240), again, paired[...])
    emb[...] = dot(again.astype(BF), w_embed[...], 0, 0)

    for i in range(5):
        forward(i * 16, STEP if i == 0 else i * 16 - 16, None if i == 0 else has_left)
        forward(
            240 if i == 4 else 128 + i * 16, STEP + 240 if i == 4 else STEP + BINS + i * 16,
            None if i == 4 else has_right,
        )

    for i in range(5):
        mix(i)
        mix(15 - i)

    halo[2].wait_recv()
    halo[3].wait_recv()
    outside = dot(rim[...], w_widen[...], 1, 1)
    dblk[0:STEP] = (outside[0:STEP] * has_left).astype(BF)
    dblk[STEP + BINS : ROWS] = (outside[STEP:] * has_right).astype(BF)

    add_up([backward(i) for k in range(5) for i in (k, 15 - k)])
    sm[0 : KE * 4] = dot(paired[...].astype(BF), half[...], 1, 0)
    for k in range(4):
        sm[KE * 4 + k : KE * 4 + k + 1] = jnp.sum(totals[k], axis=0, keepdims=True)
    for c in range(TILES):
        i, j = c // 6, c % 6
        smb[c] = sm[16 * i : 16 * i + 16, 128 * j : 128 * j + 128].astype(BF)

    rs_copies = []
    for k in range(TILES):
        c = (me + k) % TILES
        r = remote(
            smb.at[c], rsrecv.at[me], rss.at[k], rsr.at[me],
            device((c // 4) % 4, c % 4, z, c // 16),
        )
        if k == 0:
            stay = pltpu.make_async_copy(smb.at[c], rsrecv.at[me], rsr.at[me])
            pl.when(reducer)(stay.start)
            pl.when(jnp.logical_not(reducer))(r.start)
        else:
            r.start()
        rs_copies.append(r)

    core_copies = []
    for h in range(2):
        oth[h] = dot(cot_t[1, h], block[...], 1, 0).astype(BF).reshape(4, 4, 16, C0)
    for o in ORDER:
        for h in range(2):
            then = (y + o) % 4 if h == 0 else (x + o) % 4
            c = remote(
                oth.at[h, :, then], crecv.at[h, o], csem_s.at[h, o], csem_r.at[h, o],
                device(x, y, z, other),
            )
            c.start()
            core_copies.append((o, h, then, c))
    for h in range(2):
        own[h] = dot(cot_t[0, h], block[...], 1, 0).reshape(4, 4, 16, C0)

    copies1 = {}
    for o, h, then, c in core_copies:
        c.wait_recv()
        for first in ORDER:
            tgt = (x + first) % 4 if h == 0 else (y + first) % 4
            total = own[h, tgt, then] + crecv[h, o, tgt].astype(F32)
            if first == 0:
                acc1[h, o] = total
            else:
                send1[h, o, first - 1] = total.astype(BF)
                dev = device(tgt, y, z, core) if h == 0 else device(x, tgt, z, core)
                r = remote(
                    send1.at[h, o, first - 1], recv1.at[h, o, first - 1],
                    s1s.at[h, o, first - 1], s1r.at[h, o, first - 1], dev,
                )
                r.start()
                copies1[h, o, first] = r

    pl.semaphore_wait(heard.at[1], len(NEAR))

    z_small = [
        remote(
            ssend, srecv.at[dz - 1], ss.at[dz - 1], sr.at[dz - 1],
            device(x, y, (z + dz) % 16, core),
        )
        for dz in range(1, 16)
    ]

    @pl.when(reducer)
    def _():
        total = jnp.zeros((16, 128), F32)
        for k in range(32):
            remote(
                smb.at[0], rsrecv.at[k], rss.at[0], rsr.at[k], device(x, y, z, other)
            ).wait_recv()
            total = total + rsrecv[k].astype(F32)
        part[...] = total
        ssend[...] = total.astype(BF)
        for r in z_small:
            r.start()

    copies2 = {}
    for o in ORDER:
        for h in range(2):
            for first in (1, 3, 2):
                copies1[h, o, first].wait_recv()
            tgt = (y + o) % 4 if h == 0 else (x + o) % 4
            total = acc1[h, o]
            for k in range(3):
                total = total + recv1[h, o, k].astype(F32)
            if o == 0:
                acc2[h] = total
            else:
                send2[h, o - 1] = total.astype(BF)
                dev = device(x, tgt, z, core) if h == 0 else device(tgt, y, z, core)
                r = remote(
                    send2.at[h, o - 1], recv2.at[h, o - 1],
                    s2s.at[h, o - 1], s2r.at[h, o - 1], dev,
                )
                r.start()
                copies2[h, o] = r

    zcopies = []
    for h in range(2):
        for o in (1, 3, 2):
            copies2[h, o].wait_recv()
        total = acc2[h]
        for k in range(3):
            total = total + recv2[h, k].astype(F32)
        for d in range(8):
            piece = total[:, 96 * d : 96 * d + 96].astype(BF)
            zsend[h, d] = jnp.concatenate([piece, jnp.zeros((16, 32), BF)], axis=1)
            to_y, to_z = d % 4, (d // 4) * 8 + 2 * y + h
            r = remote(
                zsend.at[h, d], zrecv.at[z], zs.at[h * 8 + d], zr.at[z],
                device(x, to_y, to_z, core),
            )
            stay = pltpu.make_async_copy(zsend.at[h, d], zrecv.at[z], zr.at[z])
            mine = jnp.logical_and(to_y == y, to_z == z)
            pl.when(mine)(stay.start)
            pl.when(jnp.logical_not(mine))(r.start)
            zcopies.append((mine, r))

    gcopies = [
        remote(
            fin, agb.at[me], gs.at[k], gr.at[me],
            device((x + dx) % 4, (y + dy) % 4, z, (core + dc) % 2),
        )
        for k, (dc, dx, dy) in enumerate(PLANE)
    ]

    @pl.when(reducer)
    def _():
        total = part[...]
        for k in range(15):
            z_small[k].wait_recv()
            total = total + srecv[k].astype(F32)
        fin[...] = total.astype(BF)
        agb[me] = total.astype(BF)
        for r in gcopies:
            r.start()

    total = jnp.zeros((16, 128), F32)
    for k in range(16):
        remote(
            zsend.at[0, 0], zrecv.at[k], zs.at[0], zr.at[k], device(x, y, z, other)
        ).wait_recv()
        total = total + zrecv[k].astype(F32)
    o_widen[...] = total

    for c in range(TILES):
        r = remote(fin, agb.at[c], gs.at[0], gr.at[c], device(x, y, z, other))
        pl.when(me != c)(r.wait_recv)
    for c in halo:
        c.wait_send()
    for _, _, _, c in core_copies:
        c.wait_send()
    for c in list(copies1.values()) + list(copies2.values()) + rs_copies[1:]:
        c.wait_send()
    pl.when(jnp.logical_not(reducer))(rs_copies[0].wait_send)

    @pl.when(reducer)
    def _():
        for r in z_small + gcopies:
            r.wait_send()

    for mine, r in zcopies:
        pl.when(jnp.logical_not(mine))(r.wait_send)


def finish(agb, wid, o_embed, o_bias, o_gain, o_taps, o_widen):
    rows = []
    for i in range(4):
        rows.append(jnp.concatenate([agb[6 * i + j] for j in range(6)], axis=1).astype(F32))
    o_embed[0:48] = jnp.concatenate(rows[:3], axis=0)
    o_embed[48:60] = rows[3][0:12]
    o_bias[...] = jnp.sum(rows[1][12:16], axis=0, keepdims=True).reshape(C0)
    o_gain[...] = rows[3][12:13].reshape(C0)
    o_taps[...] = rows[3][13:16]
    o_widen[...] = wid[0:14, 0:96]


def local(bases, w_embed, b_embed, gain, taps, w_widen, cotangent):
    dma = pltpu.SemaphoreType.DMA
    vmem = pl.BlockSpec(memory_space=pltpu.VMEM)
    agb, wid = pl.pallas_call(
        kernel,
        out_shape=(
            jax.ShapeDtypeStruct((TILES, 16, 128), BF),
            jax.ShapeDtypeStruct((16, 128), F32),
        ),
        in_specs=[pl.BlockSpec(memory_space=pltpu.HBM)] * 7,
        out_specs=(vmem,) * 2,
        scratch_shapes=[
            pltpu.VMEM((1, 512), jnp.int32),
            pltpu.VMEM((KE * 4, C0), BF),
            pltpu.VMEM((C0,), F32),
            pltpu.VMEM((C0,), F32),
            pltpu.VMEM((3, C0), F32),
            pltpu.VMEM((C0, C1), BF),
            pltpu.VMEM((1, BINS, C1), BF),
            pltpu.VMEM((1, 512), jnp.int32),
            pltpu.VMEM((1, 512), jnp.int32),
            pltpu.VMEM((2 * STEP, C1), BF),
            pltpu.VMEM((16, 1024), F32),
            pltpu.VMEM((KE * 4, BINS), F32),
            pltpu.VMEM((BINS, C0), F32),
            pltpu.VMEM((ROWS, C0), BF),
            pltpu.VMEM((ROWS, C0), BF),
            pltpu.VMEM((ROWS, C0), BF),
            pltpu.VMEM((BINS, C0), BF),
            pltpu.VMEM((BINS, C0), BF),
            pltpu.VMEM((2, 2, 256, BINS), BF),
            pltpu.VMEM((64, C0), F32),
            pltpu.VMEM((TILES, 16, 128), BF),
            pltpu.VMEM((2, 4, 4, 16, C0), F32),
            pltpu.VMEM((2, 4, 4, 16, C0), BF),
            pltpu.VMEM((2, 4, 4, 16, C0), BF),
            pltpu.VMEM((2, 4, 3, 16, C0), BF),
            pltpu.VMEM((2, 4, 3, 16, C0), BF),
            pltpu.VMEM((2, 4, 16, C0), F32),
            pltpu.VMEM((2, 3, 16, C0), BF),
            pltpu.VMEM((2, 3, 16, C0), BF),
            pltpu.VMEM((2, 16, C0), F32),
            pltpu.VMEM((2, 8, 16, 128), BF),
            pltpu.VMEM((16, 16, 128), BF),
            pltpu.VMEM((32, 16, 128), BF),
            pltpu.VMEM((16, 128), F32),
            pltpu.VMEM((16, 128), BF),
            pltpu.VMEM((15, 16, 128), BF),
            pltpu.VMEM((16, 128), BF),
            pltpu.VMEM((4, 8, C0), F32),
            dma((7,)),
            pltpu.SemaphoreType.REGULAR((2,)),
            dma((4,)), dma((4,)),
            dma((2, 4)), dma((2, 4)),
            dma((2, 4, 3)), dma((2, 4, 3)),
            dma((2, 3)), dma((2, 3)),
            dma((16,)), dma((16,)),
            dma((TILES,)), dma((32,)),
            dma((15,)), dma((15,)),
            dma((31,)), dma((TILES,)),
        ],
        compiler_params=pltpu.CompilerParams(
            collective_id=0, has_side_effects=True, vmem_limit_bytes=60 * 1024 * 1024
        ),
        name="encoder_backward",
    )(bases, w_embed, b_embed, gain, taps, w_widen, cotangent)
    out = pl.pallas_call(
        finish,
        out_shape=(
            jax.ShapeDtypeStruct((KE * 4, C0), F32),
            jax.ShapeDtypeStruct((C0,), F32),
            jax.ShapeDtypeStruct((C0,), F32),
            jax.ShapeDtypeStruct((3, C0), F32),
            jax.ShapeDtypeStruct((14, 96), F32),
        ),
        in_specs=[vmem] * 2,
        out_specs=(vmem,) * 5,
        compiler_params=pltpu.CompilerParams(vmem_limit_bytes=60 * 1024 * 1024),
        name="finish",
    )(agb, wid)
    return (*out[:4], out[4].T)


def solution(mesh):
    return jax.shard_map(
        local,
        mesh=mesh,
        in_specs=(P("dp", "seq"), P(), P(), P(), P(), P(), P("dp", "seq", None)),
        out_specs=(P(), P(), P(), P(), P("dp", "seq")),
        check_vma=False,
    )
```

```python
import jax
import jax.numpy as jnp
from jax import lax
from jax.experimental import pallas as pl
from jax.experimental.pallas import tpu as pltpu
from jax.sharding import PartitionSpec as P

KE = 15
STEP = 64
C0 = 768
C1 = 896
BINS = 256
ROWS = BINS + 2 * STEP
TILES = 24
MESH = pl.DeviceIdType.MESH
BF = jnp.bfloat16
F32 = jnp.float32
ORDER = (2, 1, 3, 0)
PLANE = [(dc, dx, dy) for dx in (2, 1, 3, 0) for dy in (2, 1, 3, 0) for dc in (1, 0)][:-1]
NEAR = tuple(
    [(0, 2, 0, 0), (0, 0, 2, 0), (0, 0, 0, 2), (0, 0, 0, 14), (1, 0, 0, 0)]
    + [(0, k, 0, 0) for k in (1, 3)] + [(0, 0, k, 0) for k in (1, 3)] + [(0, 0, 0, k) for k in (1, 15)]
)
ROUNDS = (
    NEAR[:-2],
    ((0, 0, 0, 4), (0, 0, 0, 12), (1, 0, 0, 0)),
    ((0, 0, 0, 4), (0, 0, 0, 12)),
)
GELU_A = 0.7978845608028654
GELU_B = 0.044715


def device(x, y, z, core):
    return {"seq": (x * 8 + z % 8) * 2 + core, "dp": (z // 8) * 4 + y}


def dot(a, b, ca, cb):
    return lax.dot_general(a, b, (((ca,), (cb,)), ((), ())), preferred_element_type=F32)


def iota(shape, dim):
    return lax.broadcasted_iota(jnp.int32, shape, dim)


def chosen(shape, cond):
    return jnp.where(cond, jnp.ones(shape, F32), jnp.zeros(shape, F32)).astype(BF)


def column_choice(h, core):
    j = iota((256, 1), 0)
    a, b, i = j >> 6, (j >> 4) & 3, j & 15
    x, yq = (a, b) if h == 0 else (b, a)
    col = ((x * 8 + yq * 2 + h) * 2 + core) * 14 + i
    col = jnp.where(i < 14, col, -1)
    return chosen((256, C1), iota((256, C1), 1) == col)


def normed(pooled, gain):
    xf = pooled.astype(F32)
    rs = lax.rsqrt(jnp.mean(xf * xf, axis=-1, keepdims=True) + 1e-06)
    y = xf * rs
    n = y * gain
    t = jnp.tanh(GELU_A * (n + GELU_B * (n * n * n)))
    return rs, y, n, t


def fold(v):
    return v[0:8] + v[8:16]


def kernel(
    h_bases, h_embed, h_bias, h_gain, h_taps, h_widen, h_cot,
    agb, o_widen,
    bases, w_embed, b_embed, gain, taps, w_widen, cot,
    lb, rb, rim, tt, paired, emb, pool, act, dblk, block, half, cot_t, sm, smb,
    own, oth, crecv, send1, recv1, acc1, send2, recv2, acc2, zsend, zrecv,
    rsrecv, part, ssend, srecv, fin, totals,
    ins, heard, hs, hr, csem_s, csem_r, s1s, s1r, s2s, s2r, zs, zr, rss, rsr, ss, sr, gs, gr,
):
    pairs = [
        (h_bases, bases), (h_embed, w_embed), (h_bias, b_embed), (h_gain, gain),
        (h_taps, taps), (h_cot, cot), (h_widen, w_widen),
    ]
    loads = [pltpu.make_async_copy(a, b, ins.at[k]) for k, (a, b) in enumerate(pairs)]
    for c in loads:
        c.start()
    seq = lax.axis_index("seq")
    dp = lax.axis_index("dp")
    core = seq % 2
    x = seq // 16
    y = dp % 4
    z = (dp // 4) * 8 + (seq // 2) % 8
    other = 1 - core
    me = (core * 4 + x) * 4 + y
    reducer = me < TILES
    right = {"seq": (seq + 1) % 64, "dp": dp}
    left = {"seq": (seq + 63) % 64, "dp": dp}

    barrier = pltpu.get_barrier_semaphore()

    def signal(sem, dev):
        pl.semaphore_signal(sem, inc=1, device_id=dev, device_id_type=MESH)

    def near(dc, dx, dy, dz):
        return device((x + dx) % 4, (y + dy) % 4, (z + dz) % 16, (core + dc) % 2)

    signal(barrier, right)
    signal(barrier, left)
    for step in NEAR:
        signal(barrier, near(*step))

    def remote(src, dst, send, recv, dev):
        return pltpu.make_async_remote_copy(
            src_ref=src, dst_ref=dst, send_sem=send, recv_sem=recv,
            device_id=dev, device_id_type=MESH,
        )

    pl.semaphore_wait(barrier, 2 + len(NEAR))

    halo = [
        remote(h_bases, lb, hs.at[0], hr.at[0], right),
        remote(h_bases, rb, hs.at[1], hr.at[1], left),
        remote(h_cot.at[0, pl.ds(BINS - STEP, STEP)], rim.at[pl.ds(0, STEP)], hs.at[2], hr.at[2], right),
        remote(h_cot.at[0, pl.ds(0, STEP)], rim.at[pl.ds(STEP, STEP)], hs.at[3], hr.at[3], left),
    ]
    for c in halo:
        c.start()

    def pass_on(k):
        if k > 0:
            pl.semaphore_wait(heard.at[k - 1], len(ROUNDS[k - 1]))
        for step in ROUNDS[k]:
            signal(heard.at[k], near(*step))

    pass_on(0)

    p, col = iota((C0, BINS), 0), iota((C0, BINS), 1)
    tap_of, base_of = iota((KE * 4, 16), 0) >> 2, (iota((KE * 4, BINS), 0) & 3).astype(F32)
    place = iota((KE * 4, 16), 1)
    one, zero = jnp.ones((KE * 4, BINS), F32), jnp.zeros((KE * 4, BINS), F32)

    def pairs_of(ext, bins):
        for m in range(16):
            tt[m : m + 1, :] = pltpu.roll(ext, 1024 - 121 - m, 1)
        even = chosen((C0, BINS), p == 2 * bins + 128)
        win = dot(tt[:, 0:C0].astype(BF), even, 1, 0).astype(BF)
        first = dot(chosen((KE * 4, 16), place == tap_of), win, 1, 0)
        second = dot(chosen((KE * 4, 16), place == tap_of + 1), win, 1, 0)
        return jnp.where(first == base_of, one, zero) + jnp.where(second == base_of, one, zero)

    def forward(src, dst, keep):
        v = (emb[pl.ds(src, 16)] * 0.5 + b_row).astype(BF)
        pool[pl.ds(dst, 16)] = v
        _, _, n, t = normed(v, gain_row)
        a = 0.5 * n * (1.0 + t)
        act[pl.ds(dst, 16)] = (a if keep is None else a * keep).astype(BF)

    def aligned(v):
        return v if isinstance(v, int) else pl.multiple_of(v, 16)

    def mix(i):
        total = pool[pl.ds(aligned(i * 16 + STEP), 16)].astype(F32)
        for k in (1, 0, 2):
            total = total + taps[k : k + 1] * act[pl.ds(aligned(i * 16 + k * STEP), 16)].astype(F32)
        block[pl.ds(aligned(i * 16), 16)] = total.astype(BF)

    def backward(i):
        at = [pl.ds(aligned(i * 16 + k * STEP), 16) for k in range(3)]
        d = dblk[at[1]].astype(F32)
        d_act = taps[1:2] * d
        d_act = d_act + taps[0:1] * dblk[at[2]].astype(F32)
        d_act = d_act + taps[2:3] * dblk[at[0]].astype(F32)
        rs, yv, n, t = normed(pool[at[1]], gain_row)
        slope = 0.5 * (1.0 + t) + 0.5 * n * (1.0 - t * t) * (
            GELU_A * (1.0 + 3.0 * GELU_B * (n * n))
        )
        dn = d_act * slope
        dy = dn * gain_row
        d_norm = rs * (dy - yv * jnp.mean(dy * yv, axis=-1, keepdims=True))
        half[pl.ds(aligned(i * 16), 16)] = ((d + d_norm) * 0.5).astype(BF)
        return [fold(dn * yv)] + [fold(d * act[at[k]].astype(F32)) for k in range(3)]

    for c in loads[:5]:
        c.wait()
    b_row = b_embed[...].reshape(1, C0)
    gain_row = gain[...].reshape(1, C0)
    mid = bases[...].astype(F32)
    gap = jnp.full((1, 256), -1.0, F32)
    paired[...] = pairs_of(jnp.concatenate([gap, mid, gap], axis=1), col)
    emb[...] = dot(paired[...].astype(BF), w_embed[...], 0, 0)

    def own_forward(i, _):
        for k in range(4):
            at = aligned(i * 64 + 16 * k)
            forward(at, aligned(at + STEP), None)
        return 0

    lax.fori_loop(0, BINS // 64, own_forward, 0)
    loads[5].wait()

    loads[6].wait()
    dblk[STEP : STEP + BINS] = dot(cot[0], w_widen[...], 1, 1).astype(BF)
    for w in range(2):
        for h in range(2):
            pick = column_choice(h, core if w == 0 else other)
            cot_t[w, h] = dot(pick, cot[0], 1, 1).astype(BF)

    totals[...] = jnp.zeros((4, 8, C0), F32)

    def add_up(news):
        for k in range(4):
            total = totals[k]
            for new in news:
                total = total + new[k]
            totals[k] = total

    for i in range(5, 11):
        mix(i)
    add_up([backward(i) for i in range(5, 11)])

    pass_on(1)

    halo[0].wait_recv()
    halo[1].wait_recv()
    has_left = jnp.where(seq > 0, 1.0, 0.0)
    has_right = jnp.where(seq < 63, 1.0, 0.0)
    ext = jnp.concatenate([lb[:, 256:512], bases[...], rb[:, 0:256]], axis=1)
    pos = iota((1, 1024), 1) + seq * 512 - 256
    ext = jnp.where(jnp.logical_and(pos >= 0, pos < 32768), ext, -1).astype(F32)
    bins = jnp.where(
        jnp.logical_or(col < 16, col >= 240), col, jnp.where(col < 128, col - 80, col + 128)
    )
    again = pairs_of(ext, bins)
    lane = iota((KE * 4, BINS), 1)
    paired[...] = jnp.where(jnp.logical_or(lane < 16, lane >= 240), again, paired[...])
    emb[...] = dot(again.astype(BF), w_embed[...], 0, 0)

    for i in range(5):
        forward(i * 16, STEP if i == 0 else i * 16 - 16, None if i == 0 else has_left)
        forward(
            240 if i == 4 else 128 + i * 16, STEP + 240 if i == 4 else STEP + BINS + i * 16,
            None if i == 4 else has_right,
        )

    for i in range(5):
        mix(i)
        mix(15 - i)

    halo[2].wait_recv()
    halo[3].wait_recv()
    outside = dot(rim[...], w_widen[...], 1, 1)
    dblk[0:STEP] = (outside[0:STEP] * has_left).astype(BF)
    dblk[STEP + BINS : ROWS] = (outside[STEP:] * has_right).astype(BF)

    add_up([backward(i) for k in range(5) for i in (k, 15 - k)])
    sm[0 : KE * 4] = dot(paired[...].astype(BF), half[...], 1, 0)
    for k in range(4):
        sm[KE * 4 + k : KE * 4 + k + 1] = jnp.sum(totals[k], axis=0, keepdims=True)
    for c in range(TILES):
        i, j = c // 6, c % 6
        smb[c] = sm[16 * i : 16 * i + 16, 128 * j : 128 * j + 128].astype(BF)

    pass_on(2)

    rs_copies = []
    for k in range(TILES):
        c = (me + k) % TILES
        r = remote(
            smb.at[c], rsrecv.at[me], rss.at[k], rsr.at[me],
            device((c // 4) % 4, c % 4, z, c // 16),
        )
        if k == 0:
            stay = pltpu.make_async_copy(smb.at[c], rsrecv.at[me], rsr.at[me])
            pl.when(reducer)(stay.start)
            pl.when(jnp.logical_not(reducer))(r.start)
        else:
            r.start()
        rs_copies.append(r)

    core_copies = []
    for h in range(2):
        oth[h] = dot(cot_t[1, h], block[...], 1, 0).astype(BF).reshape(4, 4, 16, C0)
    for o in ORDER:
        for h in range(2):
            then = (y + o) % 4 if h == 0 else (x + o) % 4
            c = remote(
                oth.at[h, :, then], crecv.at[h, o], csem_s.at[h, o], csem_r.at[h, o],
                device(x, y, z, other),
            )
            c.start()
            core_copies.append((o, h, then, c))
    for h in range(2):
        own[h] = dot(cot_t[0, h], block[...], 1, 0).reshape(4, 4, 16, C0)

    copies1 = {}
    for o, h, then, c in core_copies:
        c.wait_recv()
        for first in ORDER:
            tgt = (x + first) % 4 if h == 0 else (y + first) % 4
            total = own[h, tgt, then] + crecv[h, o, tgt].astype(F32)
            if first == 0:
                acc1[h, o] = total
            else:
                send1[h, o, first - 1] = total.astype(BF)
                dev = device(tgt, y, z, core) if h == 0 else device(x, tgt, z, core)
                r = remote(
                    send1.at[h, o, first - 1], recv1.at[h, o, first - 1],
                    s1s.at[h, o, first - 1], s1r.at[h, o, first - 1], dev,
                )
                r.start()
                copies1[h, o, first] = r

    z_small = [
        remote(
            ssend, srecv.at[dz - 1], ss.at[dz - 1], sr.at[dz - 1],
            device(x, y, (z + dz) % 16, core),
        )
        for dz in range(1, 16)
    ]

    @pl.when(reducer)
    def _():
        total = jnp.zeros((16, 128), F32)
        for k in range(32):
            remote(
                smb.at[0], rsrecv.at[k], rss.at[0], rsr.at[k], device(x, y, z, other)
            ).wait_recv()
            total = total + rsrecv[k].astype(F32)
        part[...] = total
        ssend[...] = total.astype(BF)
        for r in z_small:
            r.start()

    copies2 = {}
    for o in ORDER:
        for h in range(2):
            for first in (1, 3, 2):
                copies1[h, o, first].wait_recv()
            tgt = (y + o) % 4 if h == 0 else (x + o) % 4
            total = acc1[h, o]
            for k in range(3):
                total = total + recv1[h, o, k].astype(F32)
            if o == 0:
                acc2[h] = total
            else:
                send2[h, o - 1] = total.astype(BF)
                dev = device(x, tgt, z, core) if h == 0 else device(tgt, y, z, core)
                r = remote(
                    send2.at[h, o - 1], recv2.at[h, o - 1],
                    s2s.at[h, o - 1], s2r.at[h, o - 1], dev,
                )
                r.start()
                copies2[h, o] = r

    pl.semaphore_wait(heard.at[2], len(ROUNDS[2]))

    zcopies = []
    for h in range(2):
        for o in (1, 3, 2):
            copies2[h, o].wait_recv()
        total = acc2[h]
        for k in range(3):
            total = total + recv2[h, k].astype(F32)
        for d in range(8):
            piece = total[:, 96 * d : 96 * d + 96].astype(BF)
            zsend[h, d] = jnp.concatenate([piece, jnp.zeros((16, 32), BF)], axis=1)
            to_y, to_z = d % 4, (d // 4) * 8 + 2 * y + h
            r = remote(
                zsend.at[h, d], zrecv.at[z], zs.at[h * 8 + d], zr.at[z],
                device(x, to_y, to_z, core),
            )
            stay = pltpu.make_async_copy(zsend.at[h, d], zrecv.at[z], zr.at[z])
            mine = jnp.logical_and(to_y == y, to_z == z)
            pl.when(mine)(stay.start)
            pl.when(jnp.logical_not(mine))(r.start)
            zcopies.append((mine, r))

    gcopies = [
        remote(
            fin, agb.at[me], gs.at[k], gr.at[me],
            device((x + dx) % 4, (y + dy) % 4, z, (core + dc) % 2),
        )
        for k, (dc, dx, dy) in enumerate(PLANE)
    ]

    @pl.when(reducer)
    def _():
        total = part[...]
        for k in range(15):
            z_small[k].wait_recv()
            total = total + srecv[k].astype(F32)
        fin[...] = total.astype(BF)
        agb[me] = total.astype(BF)
        for r in gcopies:
            r.start()

    total = jnp.zeros((16, 128), F32)
    for k in range(16):
        remote(
            zsend.at[0, 0], zrecv.at[k], zs.at[0], zr.at[k], device(x, y, z, other)
        ).wait_recv()
        total = total + zrecv[k].astype(F32)
    o_widen[...] = total

    for c in range(TILES):
        r = remote(fin, agb.at[c], gs.at[0], gr.at[c], device(x, y, z, other))
        pl.when(me != c)(r.wait_recv)
    for c in halo:
        c.wait_send()
    for _, _, _, c in core_copies:
        c.wait_send()
    for c in list(copies1.values()) + list(copies2.values()) + rs_copies[1:]:
        c.wait_send()
    pl.when(jnp.logical_not(reducer))(rs_copies[0].wait_send)

    @pl.when(reducer)
    def _():
        for r in z_small + gcopies:
            r.wait_send()

    for mine, r in zcopies:
        pl.when(jnp.logical_not(mine))(r.wait_send)


def finish(agb, wid, o_embed, o_bias, o_gain, o_taps, o_widen):
    rows = []
    for i in range(4):
        rows.append(jnp.concatenate([agb[6 * i + j] for j in range(6)], axis=1).astype(F32))
    o_embed[0:48] = jnp.concatenate(rows[:3], axis=0)
    o_embed[48:60] = rows[3][0:12]
    o_bias[...] = jnp.sum(rows[1][12:16], axis=0, keepdims=True).reshape(C0)
    o_gain[...] = rows[3][12:13].reshape(C0)
    o_taps[...] = rows[3][13:16]
    o_widen[...] = wid[0:14, 0:96]


def local(bases, w_embed, b_embed, gain, taps, w_widen, cotangent):
    dma = pltpu.SemaphoreType.DMA
    vmem = pl.BlockSpec(memory_space=pltpu.VMEM)
    agb, wid = pl.pallas_call(
        kernel,
        out_shape=(
            jax.ShapeDtypeStruct((TILES, 16, 128), BF),
            jax.ShapeDtypeStruct((16, 128), F32),
        ),
        in_specs=[pl.BlockSpec(memory_space=pltpu.HBM)] * 7,
        out_specs=(vmem,) * 2,
        scratch_shapes=[
            pltpu.VMEM((1, 512), jnp.int32),
            pltpu.VMEM((KE * 4, C0), BF),
            pltpu.VMEM((C0,), F32),
            pltpu.VMEM((C0,), F32),
            pltpu.VMEM((3, C0), F32),
            pltpu.VMEM((C0, C1), BF),
            pltpu.VMEM((1, BINS, C1), BF),
            pltpu.VMEM((1, 512), jnp.int32),
            pltpu.VMEM((1, 512), jnp.int32),
            pltpu.VMEM((2 * STEP, C1), BF),
            pltpu.VMEM((16, 1024), F32),
            pltpu.VMEM((KE * 4, BINS), F32),
            pltpu.VMEM((BINS, C0), F32),
            pltpu.VMEM((ROWS, C0), BF),
            pltpu.VMEM((ROWS, C0), BF),
            pltpu.VMEM((ROWS, C0), BF),
            pltpu.VMEM((BINS, C0), BF),
            pltpu.VMEM((BINS, C0), BF),
            pltpu.VMEM((2, 2, 256, BINS), BF),
            pltpu.VMEM((64, C0), F32),
            pltpu.VMEM((TILES, 16, 128), BF),
            pltpu.VMEM((2, 4, 4, 16, C0), F32),
            pltpu.VMEM((2, 4, 4, 16, C0), BF),
            pltpu.VMEM((2, 4, 4, 16, C0), BF),
            pltpu.VMEM((2, 4, 3, 16, C0), BF),
            pltpu.VMEM((2, 4, 3, 16, C0), BF),
            pltpu.VMEM((2, 4, 16, C0), F32),
            pltpu.VMEM((2, 3, 16, C0), BF),
            pltpu.VMEM((2, 3, 16, C0), BF),
            pltpu.VMEM((2, 16, C0), F32),
            pltpu.VMEM((2, 8, 16, 128), BF),
            pltpu.VMEM((16, 16, 128), BF),
            pltpu.VMEM((32, 16, 128), BF),
            pltpu.VMEM((16, 128), F32),
            pltpu.VMEM((16, 128), BF),
            pltpu.VMEM((15, 16, 128), BF),
            pltpu.VMEM((16, 128), BF),
            pltpu.VMEM((4, 8, C0), F32),
            dma((7,)),
            pltpu.SemaphoreType.REGULAR((3,)),
            dma((4,)), dma((4,)),
            dma((2, 4)), dma((2, 4)),
            dma((2, 4, 3)), dma((2, 4, 3)),
            dma((2, 3)), dma((2, 3)),
            dma((16,)), dma((16,)),
            dma((TILES,)), dma((32,)),
            dma((15,)), dma((15,)),
            dma((31,)), dma((TILES,)),
        ],
        compiler_params=pltpu.CompilerParams(
            collective_id=0, has_side_effects=True, vmem_limit_bytes=60 * 1024 * 1024
        ),
        name="encoder_backward",
    )(bases, w_embed, b_embed, gain, taps, w_widen, cotangent)
    out = pl.pallas_call(
        finish,
        out_shape=(
            jax.ShapeDtypeStruct((KE * 4, C0), F32),
            jax.ShapeDtypeStruct((C0,), F32),
            jax.ShapeDtypeStruct((C0,), F32),
            jax.ShapeDtypeStruct((3, C0), F32),
            jax.ShapeDtypeStruct((14, 96), F32),
        ),
        in_specs=[vmem] * 2,
        out_specs=(vmem,) * 5,
        compiler_params=pltpu.CompilerParams(vmem_limit_bytes=60 * 1024 * 1024),
        name="finish",
    )(agb, wid)
    return (*out[:4], out[4].T)


def solution(mesh):
    return jax.shard_map(
        local,
        mesh=mesh,
        in_specs=(P("dp", "seq"), P(), P(), P(), P(), P(), P("dp", "seq", None)),
        out_specs=(P(), P(), P(), P(), P("dp", "seq")),
        check_vma=False,
    )
```

```python
import jax
import jax.numpy as jnp
from jax import lax
from jax.experimental import pallas as pl
from jax.experimental.pallas import tpu as pltpu
from jax.sharding import PartitionSpec as P

KE = 15
STEP = 64
C0 = 768
C1 = 896
BINS = 256
ROWS = BINS + 2 * STEP
TILES = 24
MESH = pl.DeviceIdType.MESH
BF = jnp.bfloat16
F32 = jnp.float32
ORDER = (2, 1, 3, 0)
PLANE = [(dc, dx, dy) for dx in (2, 1, 3, 0) for dy in (2, 1, 3, 0) for dc in (1, 0)][:-1]
NEAR = tuple(
    [(0, 2, 0, 0), (0, 0, 2, 0), (0, 0, 0, 2), (0, 0, 0, 14), (1, 0, 0, 0)]
    + [(0, k, 0, 0) for k in (1, 3)] + [(0, 0, k, 0) for k in (1, 3)] + [(0, 0, 0, k) for k in (1, 15)]
)
ALONG = ((0, 0, 0, 4), (0, 0, 0, 12))
ROUNDS = (NEAR[:-2], ((1, 0, 0, 0),), ALONG, ALONG)
GELU_A = 0.7978845608028654
GELU_B = 0.044715


def device(x, y, z, core):
    return {"seq": (x * 8 + z % 8) * 2 + core, "dp": (z // 8) * 4 + y}


def dot(a, b, ca, cb):
    return lax.dot_general(a, b, (((ca,), (cb,)), ((), ())), preferred_element_type=F32)


def iota(shape, dim):
    return lax.broadcasted_iota(jnp.int32, shape, dim)


def chosen(shape, cond):
    return jnp.where(cond, jnp.ones(shape, F32), jnp.zeros(shape, F32)).astype(BF)


def column_choice(h, core):
    j = iota((256, 1), 0)
    a, b, i = j >> 6, (j >> 4) & 3, j & 15
    x, yq = (a, b) if h == 0 else (b, a)
    col = ((x * 8 + yq * 2 + h) * 2 + core) * 14 + i
    col = jnp.where(i < 14, col, -1)
    return chosen((256, C1), iota((256, C1), 1) == col)


def normed(pooled, gain):
    xf = pooled.astype(F32)
    rs = lax.rsqrt(jnp.mean(xf * xf, axis=-1, keepdims=True) + 1e-06)
    y = xf * rs
    n = y * gain
    t = jnp.tanh(GELU_A * (n + GELU_B * (n * n * n)))
    return rs, y, n, t


def fold(v):
    return v[0:8] + v[8:16]


def kernel(
    h_bases, h_embed, h_bias, h_gain, h_taps, h_widen, h_cot,
    agb, o_widen,
    bases, w_embed, b_embed, gain, taps, w_widen, cot,
    lb, rb, rim, tt, paired, emb, pool, act, dblk, block, half, cot_t, sm, smb,
    own, oth, crecv, send1, recv1, acc1, send2, recv2, acc2, zsend, zrecv,
    rsrecv, part, ssend, srecv, fin, totals,
    ins, heard, hs, hr, csem_s, csem_r, s1s, s1r, s2s, s2r, zs, zr, rss, rsr, ss, sr, gs, gr,
):
    pairs = [
        (h_bases, bases), (h_embed, w_embed), (h_bias, b_embed), (h_gain, gain),
        (h_taps, taps), (h_cot, cot), (h_widen, w_widen),
    ]
    loads = [pltpu.make_async_copy(a, b, ins.at[k]) for k, (a, b) in enumerate(pairs)]
    for c in loads:
        c.start()
    seq = lax.axis_index("seq")
    dp = lax.axis_index("dp")
    core = seq % 2
    x = seq // 16
    y = dp % 4
    z = (dp // 4) * 8 + (seq // 2) % 8
    other = 1 - core
    me = (core * 4 + x) * 4 + y
    reducer = me < TILES
    right = {"seq": (seq + 1) % 64, "dp": dp}
    left = {"seq": (seq + 63) % 64, "dp": dp}

    barrier = pltpu.get_barrier_semaphore()

    def signal(sem, dev):
        pl.semaphore_signal(sem, inc=1, device_id=dev, device_id_type=MESH)

    def near(dc, dx, dy, dz):
        return device((x + dx) % 4, (y + dy) % 4, (z + dz) % 16, (core + dc) % 2)

    signal(barrier, right)
    signal(barrier, left)
    for step in NEAR:
        signal(barrier, near(*step))

    def remote(src, dst, send, recv, dev):
        return pltpu.make_async_remote_copy(
            src_ref=src, dst_ref=dst, send_sem=send, recv_sem=recv,
            device_id=dev, device_id_type=MESH,
        )

    pl.semaphore_wait(barrier, 2 + len(NEAR))

    halo = [
        remote(h_bases, lb, hs.at[0], hr.at[0], right),
        remote(h_bases, rb, hs.at[1], hr.at[1], left),
        remote(h_cot.at[0, pl.ds(BINS - STEP, STEP)], rim.at[pl.ds(0, STEP)], hs.at[2], hr.at[2], right),
        remote(h_cot.at[0, pl.ds(0, STEP)], rim.at[pl.ds(STEP, STEP)], hs.at[3], hr.at[3], left),
    ]
    for c in halo:
        c.start()

    def tell(k):
        for step in ROUNDS[k]:
            signal(heard.at[k], near(*step))

    def hear(k):
        pl.semaphore_wait(heard.at[k], len(ROUNDS[k]))

    tell(0)

    p, col = iota((C0, BINS), 0), iota((C0, BINS), 1)
    tap_of, base_of = iota((KE * 4, 16), 0) >> 2, (iota((KE * 4, BINS), 0) & 3).astype(F32)
    place = iota((KE * 4, 16), 1)
    one, zero = jnp.ones((KE * 4, BINS), F32), jnp.zeros((KE * 4, BINS), F32)

    def pairs_of(ext, bins):
        for m in range(16):
            tt[m : m + 1, :] = pltpu.roll(ext, 1024 - 121 - m, 1)
        even = chosen((C0, BINS), p == 2 * bins + 128)
        win = dot(tt[:, 0:C0].astype(BF), even, 1, 0).astype(BF)
        first = dot(chosen((KE * 4, 16), place == tap_of), win, 1, 0)
        second = dot(chosen((KE * 4, 16), place == tap_of + 1), win, 1, 0)
        return jnp.where(first == base_of, one, zero) + jnp.where(second == base_of, one, zero)

    def forward(src, dst, keep):
        v = (emb[pl.ds(src, 16)] * 0.5 + b_row).astype(BF)
        pool[pl.ds(dst, 16)] = v
        _, _, n, t = normed(v, gain_row)
        a = 0.5 * n * (1.0 + t)
        act[pl.ds(dst, 16)] = (a if keep is None else a * keep).astype(BF)

    def aligned(v):
        return v if isinstance(v, int) else pl.multiple_of(v, 16)

    def mix(i):
        total = pool[pl.ds(aligned(i * 16 + STEP), 16)].astype(F32)
        for k in (1, 0, 2):
            total = total + taps[k : k + 1] * act[pl.ds(aligned(i * 16 + k * STEP), 16)].astype(F32)
        block[pl.ds(aligned(i * 16), 16)] = total.astype(BF)

    def backward(i):
        at = [pl.ds(aligned(i * 16 + k * STEP), 16) for k in range(3)]
        d = dblk[at[1]].astype(F32)
        d_act = taps[1:2] * d
        d_act = d_act + taps[0:1] * dblk[at[2]].astype(F32)
        d_act = d_act + taps[2:3] * dblk[at[0]].astype(F32)
        rs, yv, n, t = normed(pool[at[1]], gain_row)
        slope = 0.5 * (1.0 + t) + 0.5 * n * (1.0 - t * t) * (
            GELU_A * (1.0 + 3.0 * GELU_B * (n * n))
        )
        dn = d_act * slope
        dy = dn * gain_row
        d_norm = rs * (dy - yv * jnp.mean(dy * yv, axis=-1, keepdims=True))
        half[pl.ds(aligned(i * 16), 16)] = ((d + d_norm) * 0.5).astype(BF)
        return [fold(dn * yv)] + [fold(d * act[at[k]].astype(F32)) for k in range(3)]

    for c in loads[:5]:
        c.wait()
    b_row = b_embed[...].reshape(1, C0)
    gain_row = gain[...].reshape(1, C0)
    mid = bases[...].astype(F32)
    gap = jnp.full((1, 256), -1.0, F32)
    paired[...] = pairs_of(jnp.concatenate([gap, mid, gap], axis=1), col)
    emb[...] = dot(paired[...].astype(BF), w_embed[...], 0, 0)

    def own_forward(i, _):
        for k in range(4):
            at = aligned(i * 64 + 16 * k)
            forward(at, aligned(at + STEP), None)
        return 0

    lax.fori_loop(0, BINS // 64, own_forward, 0)
    hear(0)
    tell(1)
    tell(2)
    loads[5].wait()

    loads[6].wait()
    dblk[STEP : STEP + BINS] = dot(cot[0], w_widen[...], 1, 1).astype(BF)
    for w in range(2):
        for h in range(2):
            pick = column_choice(h, core if w == 0 else other)
            cot_t[w, h] = dot(pick, cot[0], 1, 1).astype(BF)

    totals[...] = jnp.zeros((4, 8, C0), F32)

    def add_up(news):
        for k in range(4):
            total = totals[k]
            for new in news:
                total = total + new[k]
            totals[k] = total

    for i in range(5, 11):
        mix(i)
    add_up([backward(i) for i in range(5, 11)])

    halo[0].wait_recv()
    halo[1].wait_recv()
    has_left = jnp.where(seq > 0, 1.0, 0.0)
    has_right = jnp.where(seq < 63, 1.0, 0.0)
    ext = jnp.concatenate([lb[:, 256:512], bases[...], rb[:, 0:256]], axis=1)
    pos = iota((1, 1024), 1) + seq * 512 - 256
    ext = jnp.where(jnp.logical_and(pos >= 0, pos < 32768), ext, -1).astype(F32)
    bins = jnp.where(
        jnp.logical_or(col < 16, col >= 240), col, jnp.where(col < 128, col - 80, col + 128)
    )
    again = pairs_of(ext, bins)
    lane = iota((KE * 4, BINS), 1)
    paired[...] = jnp.where(jnp.logical_or(lane < 16, lane >= 240), again, paired[...])
    emb[...] = dot(again.astype(BF), w_embed[...], 0, 0)

    for i in range(5):
        forward(i * 16, STEP if i == 0 else i * 16 - 16, None if i == 0 else has_left)
        forward(
            240 if i == 4 else 128 + i * 16, STEP + 240 if i == 4 else STEP + BINS + i * 16,
            None if i == 4 else has_right,
        )

    for i in range(5):
        mix(i)
        mix(15 - i)

    halo[2].wait_recv()
    halo[3].wait_recv()
    outside = dot(rim[...], w_widen[...], 1, 1)
    dblk[0:STEP] = (outside[0:STEP] * has_left).astype(BF)
    dblk[STEP + BINS : ROWS] = (outside[STEP:] * has_right).astype(BF)

    add_up([backward(i) for k in range(5) for i in (k, 15 - k)])
    sm[0 : KE * 4] = dot(paired[...].astype(BF), half[...], 1, 0)
    for k in range(4):
        sm[KE * 4 + k : KE * 4 + k + 1] = jnp.sum(totals[k], axis=0, keepdims=True)
    for c in range(TILES):
        i, j = c // 6, c % 6
        smb[c] = sm[16 * i : 16 * i + 16, 128 * j : 128 * j + 128].astype(BF)

    hear(1)

    rs_copies = []
    for k in range(TILES):
        c = (me + k) % TILES
        r = remote(
            smb.at[c], rsrecv.at[me], rss.at[k], rsr.at[me],
            device((c // 4) % 4, c % 4, z, c // 16),
        )
        if k == 0:
            stay = pltpu.make_async_copy(smb.at[c], rsrecv.at[me], rsr.at[me])
            pl.when(reducer)(stay.start)
            pl.when(jnp.logical_not(reducer))(r.start)
        else:
            r.start()
        rs_copies.append(r)

    core_copies = []
    for h in range(2):
        oth[h] = dot(cot_t[1, h], block[...], 1, 0).astype(BF).reshape(4, 4, 16, C0)
    for o in ORDER:
        for h in range(2):
            then = (y + o) % 4 if h == 0 else (x + o) % 4
            c = remote(
                oth.at[h, :, then], crecv.at[h, o], csem_s.at[h, o], csem_r.at[h, o],
                device(x, y, z, other),
            )
            c.start()
            core_copies.append((o, h, then, c))
    for h in range(2):
        own[h] = dot(cot_t[0, h], block[...], 1, 0).reshape(4, 4, 16, C0)

    hear(2)
    tell(3)

    copies1 = {}
    for o, h, then, c in core_copies:
        c.wait_recv()
        for first in ORDER:
            tgt = (x + first) % 4 if h == 0 else (y + first) % 4
            total = own[h, tgt, then] + crecv[h, o, tgt].astype(F32)
            if first == 0:
                acc1[h, o] = total
            else:
                send1[h, o, first - 1] = total.astype(BF)
                dev = device(tgt, y, z, core) if h == 0 else device(x, tgt, z, core)
                r = remote(
                    send1.at[h, o, first - 1], recv1.at[h, o, first - 1],
                    s1s.at[h, o, first - 1], s1r.at[h, o, first - 1], dev,
                )
                r.start()
                copies1[h, o, first] = r

    z_small = [
        remote(
            ssend, srecv.at[dz - 1], ss.at[dz - 1], sr.at[dz - 1],
            device(x, y, (z + dz) % 16, core),
        )
        for dz in range(1, 16)
    ]

    @pl.when(reducer)
    def _():
        total = jnp.zeros((16, 128), F32)
        for k in range(32):
            remote(
                smb.at[0], rsrecv.at[k], rss.at[0], rsr.at[k], device(x, y, z, other)
            ).wait_recv()
            total = total + rsrecv[k].astype(F32)
        part[...] = total
        ssend[...] = total.astype(BF)
        for r in z_small:
            r.start()

    copies2 = {}
    for o in ORDER:
        for h in range(2):
            for first in (1, 3, 2):
                copies1[h, o, first].wait_recv()
            tgt = (y + o) % 4 if h == 0 else (x + o) % 4
            total = acc1[h, o]
            for k in range(3):
                total = total + recv1[h, o, k].astype(F32)
            if o == 0:
                acc2[h] = total
            else:
                send2[h, o - 1] = total.astype(BF)
                dev = device(x, tgt, z, core) if h == 0 else device(tgt, y, z, core)
                r = remote(
                    send2.at[h, o - 1], recv2.at[h, o - 1],
                    s2s.at[h, o - 1], s2r.at[h, o - 1], dev,
                )
                r.start()
                copies2[h, o] = r

    hear(3)

    zcopies = []
    for h in range(2):
        for o in (1, 3, 2):
            copies2[h, o].wait_recv()
        total = acc2[h]
        for k in range(3):
            total = total + recv2[h, k].astype(F32)
        for d in range(8):
            piece = total[:, 96 * d : 96 * d + 96].astype(BF)
            zsend[h, d] = jnp.concatenate([piece, jnp.zeros((16, 32), BF)], axis=1)
            to_y, to_z = d % 4, (d // 4) * 8 + 2 * y + h
            r = remote(
                zsend.at[h, d], zrecv.at[z], zs.at[h * 8 + d], zr.at[z],
                device(x, to_y, to_z, core),
            )
            stay = pltpu.make_async_copy(zsend.at[h, d], zrecv.at[z], zr.at[z])
            mine = jnp.logical_and(to_y == y, to_z == z)
            pl.when(mine)(stay.start)
            pl.when(jnp.logical_not(mine))(r.start)
            zcopies.append((mine, r))

    gcopies = [
        remote(
            fin, agb.at[me], gs.at[k], gr.at[me],
            device((x + dx) % 4, (y + dy) % 4, z, (core + dc) % 2),
        )
        for k, (dc, dx, dy) in enumerate(PLANE)
    ]

    @pl.when(reducer)
    def _():
        total = part[...]
        for k in range(15):
            z_small[k].wait_recv()
            total = total + srecv[k].astype(F32)
        fin[...] = total.astype(BF)
        agb[me] = total.astype(BF)
        for r in gcopies:
            r.start()

    total = jnp.zeros((16, 128), F32)
    for k in range(16):
        remote(
            zsend.at[0, 0], zrecv.at[k], zs.at[0], zr.at[k], device(x, y, z, other)
        ).wait_recv()
        total = total + zrecv[k].astype(F32)
    o_widen[...] = total

    for c in range(TILES):
        r = remote(fin, agb.at[c], gs.at[0], gr.at[c], device(x, y, z, other))
        pl.when(me != c)(r.wait_recv)
    for c in halo:
        c.wait_send()
    for _, _, _, c in core_copies:
        c.wait_send()
    for c in list(copies1.values()) + list(copies2.values()) + rs_copies[1:]:
        c.wait_send()
    pl.when(jnp.logical_not(reducer))(rs_copies[0].wait_send)

    @pl.when(reducer)
    def _():
        for r in z_small + gcopies:
            r.wait_send()

    for mine, r in zcopies:
        pl.when(jnp.logical_not(mine))(r.wait_send)


def finish(agb, wid, o_embed, o_bias, o_gain, o_taps, o_widen):
    rows = []
    for i in range(4):
        rows.append(jnp.concatenate([agb[6 * i + j] for j in range(6)], axis=1).astype(F32))
    o_embed[0:48] = jnp.concatenate(rows[:3], axis=0)
    o_embed[48:60] = rows[3][0:12]
    o_bias[...] = jnp.sum(rows[1][12:16], axis=0, keepdims=True).reshape(C0)
    o_gain[...] = rows[3][12:13].reshape(C0)
    o_taps[...] = rows[3][13:16]
    o_widen[...] = wid[0:14, 0:96]


def local(bases, w_embed, b_embed, gain, taps, w_widen, cotangent):
    dma = pltpu.SemaphoreType.DMA
    vmem = pl.BlockSpec(memory_space=pltpu.VMEM)
    agb, wid = pl.pallas_call(
        kernel,
        out_shape=(
            jax.ShapeDtypeStruct((TILES, 16, 128), BF),
            jax.ShapeDtypeStruct((16, 128), F32),
        ),
        in_specs=[pl.BlockSpec(memory_space=pltpu.HBM)] * 7,
        out_specs=(vmem,) * 2,
        scratch_shapes=[
            pltpu.VMEM((1, 512), jnp.int32),
            pltpu.VMEM((KE * 4, C0), BF),
            pltpu.VMEM((C0,), F32),
            pltpu.VMEM((C0,), F32),
            pltpu.VMEM((3, C0), F32),
            pltpu.VMEM((C0, C1), BF),
            pltpu.VMEM((1, BINS, C1), BF),
            pltpu.VMEM((1, 512), jnp.int32),
            pltpu.VMEM((1, 512), jnp.int32),
            pltpu.VMEM((2 * STEP, C1), BF),
            pltpu.VMEM((16, 1024), F32),
            pltpu.VMEM((KE * 4, BINS), F32),
            pltpu.VMEM((BINS, C0), F32),
            pltpu.VMEM((ROWS, C0), BF),
            pltpu.VMEM((ROWS, C0), BF),
            pltpu.VMEM((ROWS, C0), BF),
            pltpu.VMEM((BINS, C0), BF),
            pltpu.VMEM((BINS, C0), BF),
            pltpu.VMEM((2, 2, 256, BINS), BF),
            pltpu.VMEM((64, C0), F32),
            pltpu.VMEM((TILES, 16, 128), BF),
            pltpu.VMEM((2, 4, 4, 16, C0), F32),
            pltpu.VMEM((2, 4, 4, 16, C0), BF),
            pltpu.VMEM((2, 4, 4, 16, C0), BF),
            pltpu.VMEM((2, 4, 3, 16, C0), BF),
            pltpu.VMEM((2, 4, 3, 16, C0), BF),
            pltpu.VMEM((2, 4, 16, C0), F32),
            pltpu.VMEM((2, 3, 16, C0), BF),
            pltpu.VMEM((2, 3, 16, C0), BF),
            pltpu.VMEM((2, 16, C0), F32),
            pltpu.VMEM((2, 8, 16, 128), BF),
            pltpu.VMEM((16, 16, 128), BF),
            pltpu.VMEM((32, 16, 128), BF),
            pltpu.VMEM((16, 128), F32),
            pltpu.VMEM((16, 128), BF),
            pltpu.VMEM((15, 16, 128), BF),
            pltpu.VMEM((16, 128), BF),
            pltpu.VMEM((4, 8, C0), F32),
            dma((7,)),
            pltpu.SemaphoreType.REGULAR((4,)),
            dma((4,)), dma((4,)),
            dma((2, 4)), dma((2, 4)),
            dma((2, 4, 3)), dma((2, 4, 3)),
            dma((2, 3)), dma((2, 3)),
            dma((16,)), dma((16,)),
            dma((TILES,)), dma((32,)),
            dma((15,)), dma((15,)),
            dma((31,)), dma((TILES,)),
        ],
        compiler_params=pltpu.CompilerParams(
            collective_id=0, has_side_effects=True, vmem_limit_bytes=60 * 1024 * 1024
        ),
        name="encoder_backward",
    )(bases, w_embed, b_embed, gain, taps, w_widen, cotangent)
    out = pl.pallas_call(
        finish,
        out_shape=(
            jax.ShapeDtypeStruct((KE * 4, C0), F32),
            jax.ShapeDtypeStruct((C0,), F32),
            jax.ShapeDtypeStruct((C0,), F32),
            jax.ShapeDtypeStruct((3, C0), F32),
            jax.ShapeDtypeStruct((14, 96), F32),
        ),
        in_specs=[vmem] * 2,
        out_specs=(vmem,) * 5,
        compiler_params=pltpu.CompilerParams(vmem_limit_bytes=60 * 1024 * 1024),
        name="finish",
    )(agb, wid)
    return (*out[:4], out[4].T)


def solution(mesh):
    return jax.shard_map(
        local,
        mesh=mesh,
        in_specs=(P("dp", "seq"), P(), P(), P(), P(), P(), P("dp", "seq", None)),
        out_specs=(P(), P(), P(), P(), P("dp", "seq")),
        check_vma=False,
    )
```
